256 devices in a mesh: expert: 16 (over x, z_lo, core), fsdp: 4 (over y), dp: 4 (over z_hi).
Axes of the slice: x: 4, y: 4, z: 8 (z_hi: 4, z_lo: 2; z = z_hi * 2 + z_lo), core: 2. Of those that a mesh axis runs over, the one named last changes fastest.
Arguments:
- inputs: bfloat16 [24576, 2048], P(('expert', 'fsdp', 'dp')), may hold values from -6 to 6
- upstream: bfloat16 [24576, 2048], P(('expert', 'fsdp', 'dp')), may hold values from -6 to 6
- gates: float32 [24576, 2], P(('expert', 'fsdp', 'dp')), may hold values from 0.2 to 1
- routes: int32 [24576, 2], P(('expert', 'fsdp', 'dp')), may hold values from 0 to 15, all different within a row; in each aligned block of 96 rows (0 to 95, 96 to 191, ...) at most 36 rows name the same one
- w_gate: bfloat16 [16, 768, 2048], P('expert', 'fsdp'), may hold values from -0.125 to 0.125
- w_up: bfloat16 [16, 768, 2048], P('expert', 'fsdp'), may hold values from -0.125 to 0.125
- w_down: bfloat16 [16, 768, 2048], P('expert', 'fsdp'), may hold values from -0.21875 to 0.21875
Outputs:
- grad_inputs: bfloat16 [24576, 2048], P(('expert', 'fsdp', 'dp'))
- grad_gate: bfloat16 [16, 768, 2048], P('expert', 'fsdp')
- grad_up: bfloat16 [16, 768, 2048], P('expert', 'fsdp')
- grad_down: bfloat16 [16, 768, 2048], P('expert', 'fsdp')
The draws below stay inside these ranges and needn't reach their ends.
Inputs may be any that keep to these rules, and one draw needn't show every extreme that they name: `routes`: each row names 2 different experts. Among the 96 rows of one device no expert is named more than 36 times, and on some device some expert is named exactly 36 times.
All inputs are finite; a program needn't handle non-finite values.
Results may differ from the reference program's by a relative error of at most 0.018.
Values may be sent and summed in bfloat16 or wider, within the bound.
A program may use at most 128 MiB of HBM per device.

```python
import math
import jax
import jax.numpy as jnp
import numpy as np
from jax import lax

D = 2048
H = 768
TOPK = 2
TOK_DEV = 96
EXPERTS = 16
CAP = 36
TOKENS = 24576
N_EXPERT = 16
N_FSDP = 4
N_DP = 4


def level_of(stream_key, shape, shards, least, high):
    factor_of = 1.0
    for dim, shards_of in shards:
        heights = jax.random.uniform(jax.random.fold_in(jax.random.fold_in(stream_key, 6), dim), (shards_of,), jnp.float32, least / len(shards), high / len(shards))
        factor_of = factor_of * jnp.repeat(jnp.exp(heights), shape[dim] // shards_of).reshape((-1,) + (1,) * (len(shape) - 1 - dim))
    return factor_of


def assign_block(stream_key, own, number, rows, amount, top, reach, skew):
    order = jax.random.permutation(stream_key, amount)
    packed, ordinary = shares(amount, rows * top, reach, skew, True), shares(amount, rows * top, reach, skew, False)
    places = jnp.arange(amount)

    def named(sizes, turn):
        used = int((sizes > 0).sum())
        fixed = max(1, used // 4)
        passed = fixed + (places - fixed + turn * (used - fixed)) % max(1, amount - fixed)
        return jnp.zeros((amount,), jnp.int32).at[order[jnp.where(places < fixed, places, passed)]].set(jnp.asarray(sizes, jnp.int32))

    sizes = jnp.where(number % 4 == 0, named(packed, number // 4), named(ordinary, number - number // 4 - 1))
    mixed = jax.random.permutation(jax.random.fold_in(own, 3), amount)
    donor, taker = mixed[0:amount // 2 * 2:2], mixed[1:amount // 2 * 2:2]
    slack = jnp.minimum(sizes[donor] - 1, reach - sizes[taker]) // 2
    slack = jnp.where((donor == order[0]) | (taker == order[0]) | (sizes[taker] == 0), 0, jnp.maximum(slack, 0))
    passed = jax.random.randint(jax.random.fold_in(own, 4), (amount // 2,), 0, 1 << 20) % (slack + 1)
    sizes = sizes.at[donor].add(-passed).at[taker].add(passed)
    labels = jnp.searchsorted(jnp.cumsum(sizes), jnp.arange(rows * top), side="right").astype(jnp.int32)
    table = labels.reshape(top, rows).T
    table = table[jax.random.permutation(jax.random.fold_in(own, 1), rows)]
    turn = jax.random.randint(jax.random.fold_in(own, 2), (rows, 1), 0, top)
    return jnp.take_along_axis(table, (jnp.arange(top)[None, :] + turn) % top, axis=1)


def shares(number_of, total, reach, skew, full):
    portions = [(1 << 20) // math.isqrt(standing ** skew) + 1 for standing in range(1, number_of + 1)]
    largest = reach if full else min(reach, max(-(-total // number_of), total * portions[0] // sum(portions)))
    least = 1 if total - largest >= number_of - 1 else 0
    given, surplus = [largest] + [least] * (number_of - 1), total - largest - least * (number_of - 1)
    while surplus > 0:
        candidates = [i for i in range(1, number_of) if given[i] < largest] or [i for i in range(1, number_of) if given[i] < reach]
        pool, budget = sum([portions[i] for i in candidates]), surplus
        for i in candidates:
            more = min(reach - given[i], max(1, budget * portions[i] // pool), surplus)
            given[i] = given[i] + more
            surplus = surplus - more
    return np.array(given)


def bell_draw(stream_key, dims, spread, reach, pieces=(), kind=jnp.bfloat16):
    drawn = jax.random.normal(stream_key, dims, jnp.float32) * spread
    if len(pieces) > 0:
        drawn = level_of(stream_key, dims, pieces, -0.22, 0.18) * drawn
    return jnp.clip(drawn, min=-reach, max=reach).astype(kind)


def setup_inputs(seed: int = 0) -> dict:
    splits = jax.random.split(jax.random.key(seed), 8)
    inputs = bell_draw(splits[0], (TOKENS, D), 1.0, 6.0, ((0, 256),))
    upstream = bell_draw(splits[1], (TOKENS, D), 1.0, 6.0, ((0, 256),))
    gates = jnp.clip(0.2 + 0.8 * jax.random.uniform(splits[2], (TOKENS, TOPK), jnp.float32) ** level_of(splits[2], (TOKENS, TOPK), ((0, 256),), -0.2, 0.2), 0.2, 1.0)
    routes_keys = jax.random.split(jax.random.fold_in(splits[3], 1), TOKENS // TOK_DEV)
    routes_turns = jax.random.permutation(jax.random.fold_in(splits[3], 3), TOKENS // TOK_DEV)
    routes = jax.vmap(lambda own, number: assign_block(jax.random.fold_in(splits[3], 2), own, number, TOK_DEV, EXPERTS, TOPK, CAP, 2))(routes_keys, routes_turns).reshape((TOKENS, TOPK))
    w_gate = bell_draw(splits[4], (EXPERTS, H, D), D ** -0.5, 0.125, ((0, 16), (1, 4)))
    w_up = bell_draw(splits[5], (EXPERTS, H, D), D ** -0.5, 0.125, ((0, 16), (1, 4)))
    w_down = bell_draw(splits[6], (EXPERTS, H, D), H ** -0.5, 0.21875, ((0, 16), (1, 4)))
    return dict(inputs=inputs, upstream=upstream, gates=gates, routes=routes, w_gate=w_gate, w_up=w_up, w_down=w_down)


def route_table(routes, experts, capacity):
    route_list = routes.reshape(-1)
    member = (route_list[:, None] == jnp.arange(experts, dtype=jnp.int32)[None, :]).astype(jnp.int32)
    earlier = jnp.cumsum(member, axis=0) - member
    position = jnp.sum(earlier * member, axis=1).astype(jnp.int32)
    target = route_list * capacity + position
    hits = jnp.arange(experts * capacity, dtype=jnp.int32)[:, None] == target[None, :]
    return hits.reshape(experts * capacity, routes.shape[0], routes.shape[1])


def dispatch(inputs, upstream, gates, routes, experts, capacity):
    hits = route_table(routes, experts, capacity)
    token_table = jnp.sum(hits.astype(jnp.int32), axis=2).astype(jnp.bfloat16)
    gate_table = jnp.sum(jnp.where(hits, gates[None, :, :], jnp.zeros_like(gates)[None, :, :]), axis=2)
    sent_inputs = jnp.dot(token_table, inputs, preferred_element_type=jnp.float32).astype(jnp.bfloat16)
    sent_scaled = jnp.dot(gate_table, upstream.astype(jnp.float32), precision=lax.Precision.HIGHEST).astype(jnp.bfloat16)
    return sent_inputs, sent_scaled, token_table


def block_backward(rows_in, rows_scaled, gate_block, up_block, down_block):
    contract_last = (((1,), (1,)), ((), ()))
    contract_first = (((0,), (0,)), ((), ()))
    gate = lax.dot_general(rows_in, gate_block, contract_last, preferred_element_type=jnp.float32)
    upward = lax.dot_general(rows_in, up_block, contract_last, preferred_element_type=jnp.float32)
    logistic = jax.nn.sigmoid(gate)
    active = gate * logistic
    slope = logistic * (1.0 + gate * (1.0 - logistic))
    hidden = (active * upward).astype(jnp.bfloat16)
    d_hidden = lax.dot_general(rows_scaled, down_block, contract_last, preferred_element_type=jnp.float32)
    d_up = (d_hidden * active).astype(jnp.bfloat16)
    d_gate = (d_hidden * upward * slope).astype(jnp.bfloat16)
    grad_down = lax.dot_general(hidden, rows_scaled, contract_first, preferred_element_type=jnp.float32)
    grad_up = lax.dot_general(d_up, rows_in, contract_first, preferred_element_type=jnp.float32)
    grad_gate = lax.dot_general(d_gate, rows_in, contract_first, preferred_element_type=jnp.float32)
    term = jnp.dot(d_gate, gate_block, preferred_element_type=jnp.float32) + jnp.dot(d_up, up_block, preferred_element_type=jnp.float32)
    return term, grad_gate, grad_up, grad_down


def rounded(value):
    return lax.optimization_barrier(value.astype(jnp.bfloat16)).astype(jnp.float32)


def reference(inputs, upstream, gates, routes, w_gate, w_up, w_down):
    device_count = N_EXPERT * N_FSDP * N_DP
    group_count = N_FSDP * N_DP
    block_h = H // N_FSDP
    row_count = N_EXPERT * CAP
    dev_inputs = inputs.reshape(device_count, TOK_DEV, D)
    dev_upstream = upstream.reshape(device_count, TOK_DEV, D)
    dev_gates = gates.reshape(device_count, TOK_DEV, TOPK)
    dev_routes = routes.reshape(device_count, TOK_DEV, TOPK)

    def one_device(dev_in, dev_up, dev_gate, dev_route):
        return dispatch(dev_in, dev_up, dev_gate, dev_route, EXPERTS, CAP)

    sent_inputs, sent_scaled, tables = jax.vmap(one_device)(dev_inputs, dev_upstream, dev_gates, dev_routes)

    def to_experts(sent):
        shaped = sent.reshape(N_EXPERT, N_FSDP, N_DP, EXPERTS, CAP, D)
        shaped = jnp.transpose(shaped, (3, 1, 2, 0, 4, 5))
        return shaped.reshape(EXPERTS, group_count, row_count, D)

    expert_inputs = to_experts(sent_inputs)
    expert_scaled = to_experts(sent_scaled)

    def one_expert(operands):
        rows_in, rows_scaled, gate_w, up_w, down_w = operands

        def one_group(totals, group):
            part_in, part_scaled = group
            d_input = jnp.zeros((row_count, D), jnp.float32)
            gate_parts, up_parts, down_parts = [], [], []
            for block_index in range(N_FSDP):
                low_row = block_index * block_h
                term, grad_g, grad_u, grad_d = block_backward(part_in, part_scaled, gate_w[low_row:low_row + block_h], up_w[low_row:low_row + block_h], down_w[low_row:low_row + block_h])
                d_input = d_input + rounded(term)
                gate_parts.append(grad_g)
                up_parts.append(grad_u)
                down_parts.append(grad_d)
            whole_gate = jnp.concatenate(gate_parts, axis=0)
            whole_up = jnp.concatenate(up_parts, axis=0)
            whole_down = jnp.concatenate(down_parts, axis=0)
            totals = (totals[0] + rounded(whole_gate), totals[1] + rounded(whole_up), totals[2] + rounded(whole_down))
            return totals, d_input.astype(jnp.bfloat16)

        empty_grad = jnp.zeros((H, D), jnp.float32)
        totals, d_rows = lax.scan(one_group, (empty_grad, empty_grad, empty_grad), (rows_in, rows_scaled))
        return totals[0].astype(jnp.bfloat16), totals[1].astype(jnp.bfloat16), totals[2].astype(jnp.bfloat16), d_rows

    grad_gate, grad_up, grad_down, d_rows = lax.map(one_expert, (expert_inputs, expert_scaled, w_gate, w_up, w_down))
    shaped = d_rows.reshape(EXPERTS, N_FSDP, N_DP, N_EXPERT, CAP, D)
    shaped = jnp.transpose(shaped, (3, 1, 2, 0, 4, 5)).reshape(device_count, EXPERTS * CAP, D)
    d_tokens = jnp.einsum("nst,nsd->ntd", tables.astype(jnp.float32), shaped.astype(jnp.float32))
    grad_inputs = d_tokens.astype(jnp.bfloat16).reshape(TOKENS, D)
    return grad_inputs, grad_gate, grad_up, grad_down
```

```python
import functools

import jax
import jax.numpy as jnp
from jax import lax
from jax.experimental import pallas as pl
from jax.experimental.pallas import tpu as pltpu
from jax.sharding import PartitionSpec as P

MESH_ID = pl.DeviceIdType.MESH
F32 = jnp.float32
BF16 = jnp.bfloat16

TOK = 96
CAP = 36
D = 2048
BLK = 192
XN = 4
GN = 4
FN = 4
DN = 4
GT = GN * TOK
CHUNK = GN * CAP
ROWS = XN * CHUNK
HALF = 2 * BLK
QUART = BLK // DN
NC = 2
CW = D // NC

NSEM = 128


def dot_nt(a, b):
    return lax.dot_general(a, b, (((1,), (1,)), ((), ())), preferred_element_type=F32)


def dot_nn(a, b):
    return lax.dot_general(a, b, (((1,), (0,)), ((), ())), preferred_element_type=F32)


def dot_tn(a, b):
    return lax.dot_general(a, b, (((0,), (0,)), ((), ())), preferred_element_type=F32)


def kernel(
    meta_ref, x_ref, u_ref, wg_ref, wu_ref, wd_ref,
    out_x, out_g, out_u, out_d,
    metas, tok, tab, gsl, snd, rows, wts, gu, dh, dgu, tr, gacc, gsend, grecv,
    red_a, red_b, red_p, red_n, fin, p_own, p_send, p_recv, q, part, core_recv,
    z_send, z_recv, gout, ssem, rsem, lsem,
):
    e = lax.axis_index("expert")
    f = lax.axis_index("fsdp")
    d = lax.axis_index("dp")
    core = lax.rem(e, 2)
    sib_e = e + 1 - 2 * core
    zp_e = e + 2 - 4 * lax.rem(lax.div(e, 2), 2)
    diag_e = zp_e + 1 - 2 * core
    near = f + 1 - 2 * lax.rem(f, 2)
    far = FN - 1 - f
    row_f = near + core * (far - near)
    wgt_f = far + core * (near - far)
    up_d = lax.rem(d + 1, DN)
    dn_d = lax.rem(d + DN - 1, DN)
    op_d = lax.rem(d + 2, DN)

    sib = {"expert": sib_e}
    zp = {"expert": zp_e}
    diag = {"expert": diag_e}
    x_at = [{"expert": lax.rem(e + GN * o, XN * GN)} for o in range(XN)]
    row_y = {"fsdp": row_f}
    wgt_y = {"fsdp": wgt_f}
    d_up = {"dp": up_d}
    d_dn = {"dp": dn_d}

    used = [0]

    def remote(src, dst, dev):
        i = used[0]
        used[0] += 1
        return pltpu.make_async_remote_copy(
            src_ref=src, dst_ref=dst, send_sem=ssem.at[i], recv_sem=rsem.at[i],
            device_id=dev, device_id_type=MESH_ID,
        )

    pending = {}

    def send(src, dst, dev):
        c = remote(src, dst, dev)
        c.start()
        pending[id(c)] = c
        return c

    lused = [0]

    def local_copy(src, dst):
        i = lused[0]
        lused[0] += 1
        c = pltpu.make_async_copy(src, dst, lsem.at[i])
        c.start()
        return c

    toks = (x_ref, u_ref)
    own_tok = [local_copy(toks[a], tok.at[a, pl.ds(0, TOK)]) for a in range(2)]
    weights = (wg_ref, wu_ref, wd_ref)
    own_wts = [local_copy(weights[m], wts.at[pl.ds(m * HALF, BLK)]) for m in range(3)]

    partners = [sib, zp, diag] + x_at[1:] + [row_y, wgt_y, d_up, d_dn]
    barrier = pltpu.get_barrier_semaphore()
    for dev in partners:
        pl.semaphore_signal(barrier, inc=1, device_id=dev, device_id_type=MESH_ID)
    pl.semaphore_wait(barrier, len(partners))

    meta_c = [send(meta_ref, metas.at[i], dev) for i, dev in enumerate((zp, sib, diag))]
    tok_z = {}
    tok_s = {}
    for a in range(2):
        for c in range(NC):
            cols = pl.ds(c * CW, CW)
            tok_z[a, c] = send(toks[a].at[:, cols], tok.at[a, pl.ds(TOK, TOK), cols], zp)
            tok_s[a, c] = send(toks[a].at[:, cols], tok.at[a, pl.ds(2 * TOK, TOK), cols], sib)
    wts_c = [
        send(weights[m], wts.at[pl.ds(m * HALF + BLK, BLK)], wgt_y) for m in range(3)
    ]

    for c in meta_c:
        c.wait_recv()
    lane = lax.broadcasted_iota(jnp.int32, (8, GT), 1)
    meta = meta_ref[...]
    for r in range(1, GN):
        meta = jnp.where(lane >= r * TOK, metas[r - 1], meta)
    source = sum((lane >= r * TOK).astype(F32) for r in range(1, GN))
    relative = lax.broadcasted_iota(jnp.int32, (8, GT), 0)
    expert = lax.rem(e + GN * relative, XN * GN).astype(F32)
    hit0 = meta[0:1] == expert
    hit1 = meta[1:2] == expert
    hit = jnp.logical_or(hit0, hit1)
    t_row = lax.broadcasted_iota(jnp.int32, (GT, GT), 0)
    t_col = lax.broadcasted_iota(jnp.int32, (GT, GT), 1)
    first = sum(jnp.where(t_col >= r * TOK, TOK, 0) for r in range(1, GN))
    before = jnp.logical_and(t_row < t_col, t_row >= first)
    earlier = dot_nn(
        jnp.where(hit, 1.0, 0.0).astype(BF16), jnp.where(before, 1.0, 0.0).astype(BF16)
    )
    target = jnp.where(hit, source * CAP + earlier, -1.0)
    weight = jnp.where(hit0, meta[2:3], jnp.where(hit1, meta[3:4], 0.0))
    slot = lax.broadcasted_iota(jnp.int32, (CHUNK, GT), 0).astype(F32)
    for o in range(XN):
        same = slot == target[o : o + 1]
        at = pl.ds(o * CHUNK, CHUNK)
        tab[at, :] = jnp.where(same, 1.0, 0.0).astype(BF16)
        gates = jnp.sum(jnp.where(same, weight[o : o + 1], 0.0), axis=1, keepdims=True)
        gsl[at, :] = jnp.broadcast_to(gates, (CHUNK, 128))

    x_c = {}
    y_c = {}

    def to_row_partner(a, c, k):
        cols = pl.ds(c * CW, CW)
        y_c[a, c, k] = send(
            rows.at[a, pl.ds(k * CHUNK, CHUNK), cols],
            rows.at[a, pl.ds(ROWS + k * CHUNK, CHUNK), cols],
            row_y,
        )

    for a in range(2):
        own_tok[a].wait()
        for c in range(NC):
            cols = pl.ds(c * CW, CW)
            tok_z[a, c].wait_recv()
            fwd = send(
                tok.at[a, pl.ds(TOK, TOK), cols], tok.at[a, pl.ds(3 * TOK, TOK), cols], sib
            )
            tok_s[a, c].wait_recv()
            fwd.wait_recv()

            @pl.loop(0, CW // 512)
            def _(n):
                tile = pl.ds(pl.multiple_of(c * CW + n * 512, 512), 512)
                picked = dot_nn(tab[...], tok[a, :, tile])
                if a == 1:
                    picked = picked * gsl[:, 0:1]
                picked = picked.astype(BF16)
                rows[a, pl.ds(0, CHUNK), tile] = picked[0:CHUNK]
                for o in range(1, XN):
                    snd[a, o - 1, :, tile] = picked[o * CHUNK : (o + 1) * CHUNK]

            for o in (2, 1, 3):
                slot_at = (XN - o) % XN
                x_c[a, c, o] = send(
                    snd.at[a, o - 1, :, cols],
                    rows.at[a, pl.ds(slot_at * CHUNK, CHUNK), cols],
                    x_at[o],
                )
            to_row_partner(a, c, 0)

    def pass_on(a, c):
        for o in (1, 3, 2):
            x_c[a, c, o].wait_recv()
            to_row_partner(a, c, (XN - o) % XN)

    def gate_up(s):
        at = pl.ds(s * ROWS, ROWS)

        @pl.loop(0, 3)
        def _(n):
            tile = pl.ds(pl.multiple_of(n * 256, 256), 256)
            gu[at, tile] = dot_nt(rows[0, at, :], wts[tile, :])

    def d_hidden(s):
        at = pl.ds(s * ROWS, ROWS)
        dh[at, :] = dot_nt(rows[1, at, :], wts[pl.ds(2 * HALF, HALF), :])

    def elementwise(low, high):
        @pl.loop(low, high)
        def _(i):
            at = pl.ds(pl.multiple_of(i * 128, 128), 128)
            gate = gu[at, pl.ds(0, HALF)]
            upward = gu[at, pl.ds(HALF, HALF)]
            dhid = dh[at, :]
            logistic = jax.nn.sigmoid(gate)
            active = gate * logistic
            slope = logistic * (1.0 + gate * (1.0 - logistic))
            hidden = (active * upward).astype(BF16)
            d_up_ = (dhid * active).astype(BF16)
            d_gate = (dhid * upward * slope).astype(BF16)
            dgu[at, pl.ds(0, HALF)] = d_gate
            dgu[at, pl.ds(HALF, HALF)] = d_up_
            for m, value in enumerate((d_gate, d_up_, hidden)):
                turned = value.T
                tr[pl.ds(m * BLK, BLK), at] = turned[BLK:HALF]
                tr[pl.ds((3 + m) * BLK, BLK), at] = turned[0:BLK]

    for c in range(NC):
        pass_on(0, c)
    for c in own_wts:
        c.wait()
    for c in wts_c:
        c.wait_recv()
    gate_up(0)
    pass_on(1, 0)
    for c in range(NC):
        for k in range(XN):
            y_c[0, c, k].wait_recv()
    gate_up(1)
    for c in range(1, NC):
        pass_on(1, c)
    d_hidden(0)
    elementwise(0, ROWS // 128)
    for c in range(NC):
        for k in range(XN):
            y_c[1, c, k].wait_recv()
    d_hidden(1)
    elementwise(ROWS // 128, 2 * ROWS // 128)

    @pl.loop(0, D // 512)
    def _(n):
        tile = pl.ds(pl.multiple_of(n * 512, 512), 512)
        value = dot_nn(tr[pl.ds(0, 2 * BLK), :], rows[0, :, tile]).astype(BF16)
        gsend[0, :, tile] = value[0:BLK]
        gsend[1, :, tile] = value[BLK : 2 * BLK]

    g_c = [send(gsend.at[m], grecv.at[m], wgt_y) for m in range(2)]

    @pl.loop(0, D // 512)
    def _(n):
        tile = pl.ds(pl.multiple_of(n * 512, 512), 512)
        gsend[2, :, tile] = dot_nn(tr[pl.ds(2 * BLK, BLK), :], rows[1, :, tile]).astype(BF16)

    g_c.append(send(gsend.at[2], grecv.at[2], wgt_y))

    p_c = []
    for c in range(NC):

        @pl.loop(0, CW // 512)
        def _(n):
            tile = pl.ds(pl.multiple_of(c * CW + n * 512, 512), 512)
            p_send[:, tile] = dot_nn(
                dgu[pl.ds(ROWS, ROWS), :], wts[pl.ds(0, 2 * HALF), tile]
            ).astype(BF16)

        cols = pl.ds(c * CW, CW)
        p_c.append(send(p_send.at[:, cols], p_recv.at[:, cols], row_y))

    @pl.loop(0, D // 512)
    def _(n):
        tile = pl.ds(pl.multiple_of(n * 512, 512), 512)
        value = dot_nn(tr[pl.ds(3 * BLK, 2 * BLK), :], rows[0, :, tile])
        gacc[0, :, tile] = value[0:BLK]
        gacc[1, :, tile] = value[BLK : 2 * BLK]
        gacc[2, :, tile] = dot_nn(tr[pl.ds(5 * BLK, BLK), :], rows[1, :, tile])

    lo = pl.ds(0, D // 2)
    hi = pl.ds(D // 2, D // 2)

    def quarter(i):
        return pl.ds(pl.multiple_of(i * QUART, QUART), QUART)

    r1 = {}
    r2 = {}
    a1 = {}
    a2 = {}

    def reduce_first(m):
        g_c[m].wait_recv()
        g_c[m].wait_send()
        del pending[id(g_c[m])]

        @pl.loop(0, BLK // 16)
        def _(i):
            at = pl.ds(pl.multiple_of(i * 16, 16), 16)
            gsend[m, at, :] = (gacc[m, at, :] + grecv[m, at, :].astype(F32)).astype(BF16)

        r1[m] = (
            send(gsend.at[m, quarter(op_d), lo], red_a.at[m], d_up),
            send(gsend.at[m, quarter(op_d), hi], red_b.at[m], d_dn),
        )

    def reduce_second(m):
        r1[m][0].wait_recv()
        at = quarter(up_d)
        gsend[m, at, lo] = (gsend[m, at, lo].astype(F32) + red_a[m].astype(F32)).astype(BF16)
        first_c = send(gsend.at[m, at, :], red_p.at[m], d_up)
        r1[m][1].wait_recv()
        at = quarter(dn_d)
        gsend[m, at, hi] = (gsend[m, at, hi].astype(F32) + red_b[m].astype(F32)).astype(BF16)
        r2[m] = (first_c, send(gsend.at[m, at, :], red_n.at[m], d_dn))

    def gather_first(m):
        r2[m][0].wait_recv()
        r2[m][1].wait_recv()
        at = quarter(d)
        fin[m, at, :] = (
            gsend[m, at, :].astype(F32) + red_p[m].astype(F32) + red_n[m].astype(F32)
        ).astype(BF16)
        a1[m] = (
            send(fin.at[m, at, :], fin.at[m, at, :], d_up),
            send(fin.at[m, at, :], fin.at[m, at, :], d_dn),
        )

    def gather_second(m):
        a1[m][0].wait_recv()
        at = quarter(dn_d)
        first_c = send(fin.at[m, at, lo], fin.at[m, at, lo], d_up)
        a1[m][1].wait_recv()
        at = quarter(up_d)
        a2[m] = (first_c, send(fin.at[m, at, hi], fin.at[m, at, hi], d_dn))

    outs = (out_g, out_u, out_d)
    done = []

    def finish(m):
        a2[m][0].wait_recv()
        a2[m][1].wait_recv()
        done.append(local_copy(fin.at[m], outs[m]))

    q_c = {}
    s_c = {}
    z_c = {}

    def return_rows(c):
        cols = pl.ds(c * CW, CW)
        p_c[c].wait_recv()
        p_c[c].wait_send()
        del pending[id(p_c[c])]

        @pl.loop(0, ROWS // 48)
        def _(i):
            at = pl.ds(pl.multiple_of(i * 48, 48), 48)
            p_send[at, cols] = (p_own[at, cols] + p_recv[at, cols].astype(F32)).astype(BF16)

        for k in (2, 1, 3):
            q_c[c, k] = send(
                p_send.at[pl.ds(k * CHUNK, CHUNK), cols],
                q.at[pl.ds((XN - k) % XN * CHUNK, CHUNK), cols],
                x_at[k],
            )
        q[pl.ds(0, CHUNK), cols] = p_send[pl.ds(0, CHUNK), cols]

    def combine(c):
        cols = pl.ds(c * CW, CW)
        for k in (1, 3, 2):
            q_c[c, k].wait_recv()

        @pl.loop(0, CW // 512)
        def _(n):
            tile = pl.ds(pl.multiple_of(c * CW + n * 512, 512), 512)
            part[:, tile] = dot_tn(tab[...], q[:, tile]).astype(BF16)

        s_c[c] = send(part.at[pl.ds(2 * TOK, 2 * TOK), cols], core_recv.at[:, cols], sib)

    def along_z(c):
        cols = pl.ds(c * CW, CW)
        s_c[c].wait_recv()
        z_send[:, cols] = (
            part[pl.ds(TOK, TOK), cols].astype(F32)
            + core_recv[pl.ds(TOK, TOK), cols].astype(F32)
        ).astype(BF16)
        z_c[c] = send(z_send.at[:, cols], z_recv.at[:, cols], zp)

    def tokens_out(c):
        cols = pl.ds(c * CW, CW)
        z_c[c].wait_recv()
        gout[:, cols] = (
            part[pl.ds(0, TOK), cols].astype(F32)
            + core_recv[pl.ds(0, TOK), cols].astype(F32)
            + z_recv[:, cols].astype(F32)
        ).astype(BF16)
        done.append(local_copy(gout.at[:, cols], out_x.at[:, cols]))

    reduce_first(0)

    @pl.loop(0, D // 512)
    def _(n):
        tile = pl.ds(pl.multiple_of(n * 512, 512), 512)
        p_own[:, tile] = dot_nn(dgu[pl.ds(0, ROWS), :], wts[pl.ds(0, 2 * HALF), tile])

    reduce_first(1)
    reduce_second(0)
    reduce_first(2)
    reduce_second(1)
    gather_first(0)
    return_rows(0)
    reduce_second(2)
    gather_second(0)
    gather_first(1)
    return_rows(1)
    gather_first(2)
    gather_second(1)
    finish(0)
    combine(0)
    along_z(0)
    gather_second(2)
    finish(1)
    combine(1)
    along_z(1)
    tokens_out(0)
    tokens_out(1)
    finish(2)
    for c in done:
        c.wait()
    for c in pending.values():
        c.wait_send()


SCRATCH = (
    ((GN - 1, 8, GT), F32),
    ((2, GT, D), BF16),
    ((ROWS, GT), BF16),
    ((ROWS, 128), F32),
    ((2, XN - 1, CHUNK, D), BF16),
    ((2, 2 * ROWS, D), BF16),
    ((3 * HALF, D), BF16),
    ((2 * ROWS, 2 * HALF), F32),
    ((2 * ROWS, HALF), F32),
    ((2 * ROWS, 2 * HALF), BF16),
    ((6 * BLK, 2 * ROWS), BF16),
    ((3, BLK, D), F32),
    ((3, BLK, D), BF16),
    ((3, BLK, D), BF16),
    ((3, QUART, D // 2), BF16),
    ((3, QUART, D // 2), BF16),
    ((3, QUART, D), BF16),
    ((3, QUART, D), BF16),
    ((3, BLK, D), BF16),
    ((ROWS, D), F32),
    ((ROWS, D), BF16),
    ((ROWS, D), BF16),
    ((ROWS, D), BF16),
    ((GT, D), BF16),
    ((2 * TOK, D), BF16),
    ((TOK, D), BF16),
    ((TOK, D), BF16),
    ((TOK, D), BF16),
)


def local(inputs, upstream, gates, routes, w_gate, w_up, w_down):
    meta = jnp.concatenate(
        [routes.T.astype(F32), gates.T, jnp.zeros((4, TOK), F32)], axis=0
    )
    meta = jnp.tile(meta, (1, GN))
    anywhere = pl.BlockSpec(memory_space=pl.ANY)
    outs = pl.pallas_call(
        kernel,
        out_shape=(
            jax.ShapeDtypeStruct((TOK, D), BF16),
            jax.ShapeDtypeStruct((BLK, D), BF16),
            jax.ShapeDtypeStruct((BLK, D), BF16),
            jax.ShapeDtypeStruct((BLK, D), BF16),
        ),
        in_specs=[pl.BlockSpec(memory_space=pltpu.VMEM)] + [anywhere] * 5,
        out_specs=[anywhere] * 4,
        scratch_shapes=[pltpu.VMEM(shape, dtype) for shape, dtype in SCRATCH]
        + [
            pltpu.SemaphoreType.DMA((NSEM,)),
            pltpu.SemaphoreType.DMA((NSEM,)),
            pltpu.SemaphoreType.DMA((16,)),
        ],
        compiler_params=pltpu.CompilerParams(
            collective_id=0, has_side_effects=True, vmem_limit_bytes=62 * 2**20
        ),
        name="expert_backward",
    )(meta, inputs, upstream, w_gate[0], w_up[0], w_down[0])
    return outs[0], outs[1][None], outs[2][None], outs[3][None]


def solution(mesh):
    tokens = P(("expert", "fsdp", "dp"), None)
    hidden = P("expert", "fsdp", None)
    return jax.shard_map(
        local,
        mesh=mesh,
        in_specs=(tokens, tokens, tokens, tokens, hidden, hidden, hidden),
        out_specs=(tokens, hidden, hidden, hidden),
        check_vma=False,
    )
```

```python
import functools

import jax
import jax.numpy as jnp
from jax import lax
from jax.experimental import pallas as pl
from jax.experimental.pallas import tpu as pltpu
from jax.sharding import PartitionSpec as P

MESH_ID = pl.DeviceIdType.MESH
F32 = jnp.float32
BF16 = jnp.bfloat16

TOK = 96
CAP = 36
D = 2048
BLK = 192
XN = 4
GN = 4
FN = 4
DN = 4
GT = GN * TOK
CHUNK = GN * CAP
ROWS = XN * CHUNK
HALF = 2 * BLK
QUART = BLK // DN
NC = 4
CW = D // NC

NSEM = 192
SPREAD = (2,)


def dot_nt(a, b):
    return lax.dot_general(a, b, (((1,), (1,)), ((), ())), preferred_element_type=F32)


def dot_nn(a, b):
    return lax.dot_general(a, b, (((1,), (0,)), ((), ())), preferred_element_type=F32)


def dot_tn(a, b):
    return lax.dot_general(a, b, (((0,), (0,)), ((), ())), preferred_element_type=F32)


def kernel(
    meta_ref, x_ref, u_ref, wg_ref, wu_ref, wd_ref,
    out_x, out_g, out_u, out_d,
    metas, tok, tab, gsl, snd, rows, wts, gu, dh, dgu, tr, gacc, gsend, grecv,
    red_a, red_b, red_p, red_n, fin, p_own, p_send, p_recv, q, part, core_recv,
    z_send, z_recv, gout, ssem, rsem, lsem,
):
    e = lax.axis_index("expert")
    f = lax.axis_index("fsdp")
    d = lax.axis_index("dp")
    core = lax.rem(e, 2)
    sib_e = e + 1 - 2 * core
    zp_e = e + 2 - 4 * lax.rem(lax.div(e, 2), 2)
    diag_e = zp_e + 1 - 2 * core
    near = f + 1 - 2 * lax.rem(f, 2)
    far = FN - 1 - f
    row_f = near + core * (far - near)
    wgt_f = far + core * (near - far)
    up_d = lax.rem(d + 1, DN)
    dn_d = lax.rem(d + DN - 1, DN)
    op_d = lax.rem(d + 2, DN)

    sib = {"expert": sib_e}
    zp = {"expert": zp_e}
    diag = {"expert": diag_e}
    x_at = [{"expert": lax.rem(e + GN * o, XN * GN)} for o in range(XN)]
    row_y = {"fsdp": row_f}
    wgt_y = {"fsdp": wgt_f}
    d_up = {"dp": up_d}
    d_dn = {"dp": dn_d}

    used = [0]

    def remote(src, dst, dev):
        i = used[0]
        used[0] += 1
        return pltpu.make_async_remote_copy(
            src_ref=src, dst_ref=dst, send_sem=ssem.at[i], recv_sem=rsem.at[i],
            device_id=dev, device_id_type=MESH_ID,
        )

    pending = {}

    def send(src, dst, dev):
        c = remote(src, dst, dev)
        c.start()
        pending[id(c)] = c
        return c

    lused = [0]

    def local_copy(src, dst):
        i = lused[0]
        lused[0] += 1
        c = pltpu.make_async_copy(src, dst, lsem.at[i])
        c.start()
        return c

    toks = (x_ref, u_ref)
    own_tok = [local_copy(toks[a], tok.at[a, pl.ds(0, TOK)]) for a in range(2)]
    weights = (wg_ref, wu_ref, wd_ref)
    own_wts = [local_copy(weights[m], wts.at[pl.ds(m * HALF, BLK)]) for m in range(3)]

    partners = [sib, zp, diag] + x_at[1:] + [row_y, wgt_y, d_up, d_dn]
    barrier = pltpu.get_barrier_semaphore()
    for dev in partners:
        pl.semaphore_signal(barrier, inc=1, device_id=dev, device_id_type=MESH_ID)
    pl.semaphore_wait(barrier, len(partners))

    def quarter(i):
        return pl.ds(pl.multiple_of(i * QUART, QUART), QUART)

    def wts_quarter(m, i):
        return pl.ds(pl.multiple_of(m * HALF + BLK + i * QUART, QUART), QUART)

    meta_c = [send(meta_ref, metas.at[i], dev) for i, dev in enumerate((zp, sib, diag))]
    tok_z = {}
    tok_s = {}

    def send_tokens(a, c):
        cols = pl.ds(c * CW, CW)
        mine = tok.at[a, pl.ds(0, TOK), cols]
        tok_z[a, c] = send(mine, tok.at[a, pl.ds(TOK, TOK), cols], zp)
        tok_s[a, c] = send(mine, tok.at[a, pl.ds(2 * TOK, TOK), cols], sib)

    steps = [(a, c) for a in range(2) for c in range(NC)]
    own_tok[0].wait()
    for step in steps[:2]:
        send_tokens(*step)
    own_tok[1].wait()
    w_y = {}
    for m in range(3):
        own_wts[m].wait()
        if m in SPREAD:
            src = wts.at[pl.ds(pl.multiple_of(m * HALF + d * QUART, QUART), QUART), :]
            w_y[m] = send(src, wts.at[wts_quarter(m, d), :], wgt_y)
        else:
            src = wts.at[pl.ds(m * HALF, BLK)]
            w_y[m] = send(src, wts.at[pl.ds(m * HALF + BLK, BLK)], wgt_y)
    w1 = {}
    w2 = {}
    lo = pl.ds(0, D // 2)
    hi = pl.ds(D // 2, D // 2)

    def weights_first(m):
        w_y[m].wait_recv()
        at = wts_quarter(m, d)
        w1[m] = (
            send(wts.at[at, :], wts.at[at, :], d_up),
            send(wts.at[at, :], wts.at[at, :], d_dn),
        )

    def weights_second(m):
        w1[m][0].wait_recv()
        at = wts_quarter(m, dn_d)
        first_c = send(wts.at[at, lo], wts.at[at, lo], d_up)
        w1[m][1].wait_recv()
        at = wts_quarter(m, up_d)
        w2[m] = (first_c, send(wts.at[at, hi], wts.at[at, hi], d_dn))

    for c in meta_c:
        c.wait_recv()
    lane = lax.broadcasted_iota(jnp.int32, (8, GT), 1)
    meta = meta_ref[...]
    for r in range(1, GN):
        meta = jnp.where(lane >= r * TOK, metas[r - 1], meta)
    source = sum((lane >= r * TOK).astype(F32) for r in range(1, GN))
    relative = lax.broadcasted_iota(jnp.int32, (8, GT), 0)
    expert = lax.rem(e + GN * relative, XN * GN).astype(F32)
    hit0 = meta[0:1] == expert
    hit1 = meta[1:2] == expert
    hit = jnp.logical_or(hit0, hit1)
    t_row = lax.broadcasted_iota(jnp.int32, (GT, GT), 0)
    t_col = lax.broadcasted_iota(jnp.int32, (GT, GT), 1)
    first = sum(jnp.where(t_col >= r * TOK, TOK, 0) for r in range(1, GN))
    before = jnp.logical_and(t_row < t_col, t_row >= first)
    earlier = dot_nn(
        jnp.where(hit, 1.0, 0.0).astype(BF16), jnp.where(before, 1.0, 0.0).astype(BF16)
    )
    target = jnp.where(hit, source * CAP + earlier, -1.0)
    weight = jnp.where(hit0, meta[2:3], jnp.where(hit1, meta[3:4], 0.0))
    slot = lax.broadcasted_iota(jnp.int32, (CHUNK, GT), 0).astype(F32)
    for o in range(XN):
        same = slot == target[o : o + 1]
        at = pl.ds(o * CHUNK, CHUNK)
        tab[at, :] = jnp.where(same, 1.0, 0.0).astype(BF16)
        gates = jnp.sum(jnp.where(same, weight[o : o + 1], 0.0), axis=1, keepdims=True)
        gsl[at, :] = jnp.broadcast_to(gates, (CHUNK, 128))

    x_c = {}
    y_c = {}

    def pick(a, c):
        cols = pl.ds(c * CW, CW)
        picked = dot_nn(tab[...], tok[a, :, cols])
        if a == 1:
            picked = picked * gsl[:, 0:1]
        picked = picked.astype(BF16)
        rows[a, pl.ds(0, CHUNK), cols] = picked[0:CHUNK]
        for o in range(1, XN):
            snd[a, o - 1, :, cols] = picked[o * CHUNK : (o + 1) * CHUNK]

    def send_rows(a, c):
        cols = pl.ds(c * CW, CW)
        for o in (2, 1, 3):
            x_c[a, c, o] = send(
                snd.at[a, o - 1, :, cols],
                rows.at[a, pl.ds((XN - o) * CHUNK, CHUNK), cols],
                x_at[o],
            )

    def pass_on(a, c):
        for o in (1, 3, 2):
            x_c[a, c, o].wait_recv()
        cols = pl.ds(c * CW, CW)
        y_c[a, c] = send(
            rows.at[a, pl.ds(0, ROWS), cols], rows.at[a, pl.ds(ROWS, ROWS), cols], row_y
        )

    def gate_up(s):
        at = pl.ds(s * ROWS, ROWS)

        @pl.loop(0, 3)
        def _(n):
            tile = pl.ds(pl.multiple_of(n * 256, 256), 256)
            gu[at, tile] = dot_nt(rows[0, at, :], wts[tile, :])

    def d_hidden(s):
        if s == 1:
            for c in range(NC):
                need(c)
        at = pl.ds(s * ROWS, ROWS)
        dh[at, :] = dot_nt(rows[1, at, :], wts[pl.ds(2 * HALF, HALF), :])

    def turn(m, at, value):
        turned = value.T
        tr[pl.ds(m * BLK, BLK), at] = turned[BLK:HALF]
        tr[pl.ds((3 + m) * BLK, BLK), at] = turned[0:BLK]

    def make_hidden():
        @pl.loop(0, 2 * ROWS // 128)
        def _(i):
            at = pl.ds(pl.multiple_of(i * 128, 128), 128)
            gate = gu[at, pl.ds(0, HALF)]
            upward = gu[at, pl.ds(HALF, HALF)]
            logistic = jax.nn.sigmoid(gate)
            active = gate * logistic
            slope = logistic * (1.0 + gate * (1.0 - logistic))
            gu[at, pl.ds(0, HALF)] = upward * slope
            gu[at, pl.ds(HALF, HALF)] = active
            turn(2, at, (active * upward).astype(BF16))

    def elementwise(low, high):
        @pl.loop(low, high)
        def _(i):
            at = pl.ds(pl.multiple_of(i * 128, 128), 128)
            dhid = dh[at, :]
            for m in range(2):
                cols = pl.ds(m * HALF, HALF)
                value = (dhid * gu[at, cols]).astype(BF16)
                dgu[at, cols] = value
                turn(m, at, value)

    def wait_weights(m):
        for c in w2[m] if m in SPREAD else (w_y[m],):
            c.wait_recv()

    for k, (a, c) in enumerate(steps):
        if k + 2 < len(steps):
            send_tokens(*steps[k + 2])
        cols = pl.ds(c * CW, CW)
        tok_z[a, c].wait_recv()
        fwd = send(tok.at[a, pl.ds(TOK, TOK), cols], tok.at[a, pl.ds(3 * TOK, TOK), cols], sib)
        tok_s[a, c].wait_recv()
        fwd.wait_recv()
        pick(a, c)
        if k >= 2:
            pass_on(*steps[k - 2])
        send_rows(a, c)
        for m in SPREAD:
            if k == 2 + m:
                weights_first(m)
            if k == 5 + m:
                weights_second(m)
        if k == NC + 2:
            for m in range(2):
                wait_weights(m)
            gate_up(0)
        if k == NC + 3:
            for i in range(NC):
                y_c[0, i].wait_recv()
            gate_up(1)

    parts = [(2, c * CW, CW) for c in range(NC)]
    half_d = D // 2
    parts += [(m, h * half_d, half_d) for h in range(2) for m in range(2)]

    landed = set()

    def need(c):
        if c not in landed:
            y_c[1, c].wait_recv()
            landed.add(c)

    def grads_down(c):
        need(c)
        cols = pl.ds(c * CW, CW)
        gsend[2, :, cols] = dot_nn(tr[pl.ds(2 * BLK, BLK), :], rows[1, :, cols]).astype(BF16)
        send_grads(c)
        gacc[2, :, cols] = dot_nn(tr[pl.ds(5 * BLK, BLK), :], rows[1, :, cols])

    def grads(mine, h):
        @pl.loop(0, half_d // 512)
        def _(n):
            tile = pl.ds(pl.multiple_of(h * half_d + n * 512, 512), 512)
            value = dot_nn(tr[pl.ds(3 * BLK * mine, 2 * BLK), :], rows[0, :, tile])
            for i in range(2):
                one = value[i * BLK : (i + 1) * BLK]
                if mine:
                    gacc[i, :, tile] = one
                else:
                    gsend[i, :, tile] = one.astype(BF16)

    g_c = {}

    def send_grads(j):
        m, low, width = parts[j]
        cols = pl.ds(low, width)
        g_c[j] = send(gsend.at[m, :, cols], grecv.at[m, :, cols], wgt_y)

    p_c = {}

    def partner_rows(c):
        @pl.loop(0, half_d // 512)
        def _(n):
            tile = pl.ds(pl.multiple_of(c * half_d + n * 512, 512), 512)
            p_send[:, tile] = dot_nn(
                dgu[pl.ds(ROWS, ROWS), :], wts[pl.ds(0, 2 * HALF), tile]
            ).astype(BF16)

    def send_partner_rows(c):
        cols = pl.ds(c * half_d, half_d)
        p_c[c] = send(p_send.at[:, cols], p_recv.at[:, cols], row_y)

    r1 = {}
    r2 = {}
    a1 = {}
    a2 = {}

    def split(j):
        m, low, width = parts[j]
        half = width // 2
        return (
            m, pl.ds(low, half), pl.ds(low + half, half), pl.ds(low, width),
            pl.ds(0, half), pl.ds(0, width),
        )

    def reduce_first(j):
        m, low, high, cols, narrow, wide = split(j)
        g_c[j].wait_recv()
        g_c[j].wait_send()
        del pending[id(g_c[j])]

        @pl.loop(0, BLK // 16)
        def _(i):
            at = pl.ds(pl.multiple_of(i * 16, 16), 16)
            gsend[m, at, cols] = (
                gacc[m, at, cols] + grecv[m, at, cols].astype(F32)
            ).astype(BF16)

        r1[j] = (
            send(gsend.at[m, quarter(op_d), low], red_a.at[j, :, narrow], d_up),
            send(gsend.at[m, quarter(op_d), high], red_b.at[j, :, narrow], d_dn),
        )

    def reduce_second(j):
        m, low, high, cols, narrow, wide = split(j)
        r1[j][0].wait_recv()
        at = quarter(up_d)
        gsend[m, at, low] = (gsend[m, at, low].astype(F32) + red_a[j, :, narrow].astype(F32)).astype(BF16)
        first_c = send(gsend.at[m, at, cols], red_p.at[j, :, wide], d_up)
        r1[j][1].wait_recv()
        at = quarter(dn_d)
        gsend[m, at, high] = (gsend[m, at, high].astype(F32) + red_b[j, :, narrow].astype(F32)).astype(BF16)
        r2[j] = (first_c, send(gsend.at[m, at, cols], red_n.at[j, :, wide], d_dn))

    def gather_first(j):
        m, low, high, cols, narrow, wide = split(j)
        r2[j][0].wait_recv()
        r2[j][1].wait_recv()
        at = quarter(d)
        fin[m, at, cols] = (
            gsend[m, at, cols].astype(F32) + red_p[j, :, wide].astype(F32) + red_n[j, :, wide].astype(F32)
        ).astype(BF16)
        a1[j] = (
            send(fin.at[m, at, cols], fin.at[m, at, cols], d_up),
            send(fin.at[m, at, cols], fin.at[m, at, cols], d_dn),
        )

    def gather_second(j):
        m, low, high, cols, narrow, wide = split(j)
        a1[j][0].wait_recv()
        at = quarter(dn_d)
        first_c = send(fin.at[m, at, low], fin.at[m, at, low], d_up)
        a1[j][1].wait_recv()
        at = quarter(up_d)
        a2[j] = (first_c, send(fin.at[m, at, high], fin.at[m, at, high], d_dn))

    outs = (out_g, out_u, out_d)
    done = []

    def finish(j):
        m, low, high, cols, narrow, wide = split(j)
        a2[j][0].wait_recv()
        a2[j][1].wait_recv()
        done.append(local_copy(fin.at[m, :, cols], outs[m].at[:, cols]))

    q_c = {}
    s_c = {}
    z_c = {}

    def own_rows():
        @pl.loop(0, D // 512)
        def _(n):
            tile = pl.ds(pl.multiple_of(n * 512, 512), 512)
            p_own[:, tile] = dot_nn(dgu[pl.ds(0, ROWS), :], wts[pl.ds(0, 2 * HALF), tile])

    def return_rows(c):
        cols = pl.ds(c * half_d, half_d)
        p_c[c].wait_recv()
        p_c[c].wait_send()
        del pending[id(p_c[c])]

        @pl.loop(0, ROWS // 48)
        def _(i):
            at = pl.ds(pl.multiple_of(i * 48, 48), 48)
            p_send[at, cols] = (p_own[at, cols] + p_recv[at, cols].astype(F32)).astype(BF16)

        for k in (2, 1, 3):
            q_c[c, k] = send(
                p_send.at[pl.ds(k * CHUNK, CHUNK), cols],
                q.at[pl.ds((XN - k) * CHUNK, CHUNK), cols],
                x_at[k],
            )
        q[pl.ds(0, CHUNK), cols] = p_send[pl.ds(0, CHUNK), cols]

    def combine(c):
        cols = pl.ds(c * half_d, half_d)
        for k in (1, 3, 2):
            q_c[c, k].wait_recv()

        @pl.loop(0, half_d // 512)
        def _(n):
            tile = pl.ds(pl.multiple_of(c * half_d + n * 512, 512), 512)
            part[:, tile] = dot_tn(tab[...], q[:, tile]).astype(BF16)

        s_c[c] = send(part.at[pl.ds(2 * TOK, 2 * TOK), cols], core_recv.at[:, cols], sib)

    def along_z(c):
        cols = pl.ds(c * half_d, half_d)
        s_c[c].wait_recv()
        z_send[:, cols] = (
            part[pl.ds(TOK, TOK), cols].astype(F32)
            + core_recv[pl.ds(TOK, TOK), cols].astype(F32)
        ).astype(BF16)
        z_c[c] = send(z_send.at[:, cols], z_recv.at[:, cols], zp)

    def tokens_out(c):
        cols = pl.ds(c * half_d, half_d)
        z_c[c].wait_recv()
        gout[:, cols] = (
            part[pl.ds(0, TOK), cols].astype(F32)
            + core_recv[pl.ds(0, TOK), cols].astype(F32)
            + z_recv[:, cols].astype(F32)
        ).astype(BF16)
        done.append(local_copy(gout.at[:, cols], out_x.at[:, cols]))

    wait_weights(2)
    make_hidden()
    grads_down(0)
    pass_on(*steps[-2])
    grads_down(1)
    reduce_first(0)
    reduce_second(0)
    pass_on(*steps[-1])
    d_hidden(0)
    reduce_first(1)
    gather_first(0)
    reduce_second(1)
    gather_second(0)
    grads_down(2)
    elementwise(0, ROWS // 128)
    gather_first(1)
    d_hidden(1)
    reduce_first(2)
    grads_down(3)
    gather_second(1)
    elementwise(ROWS // 128, 2 * ROWS // 128)
    reduce_second(2)
    grads(0, 0)
    send_grads(4)
    reduce_first(3)
    gather_first(2)
    grads(1, 0)
    reduce_second(3)
    send_grads(5)
    partner_rows(1)
    gather_second(2)
    reduce_first(4)
    partner_rows(0)
    gather_first(3)
    send_partner_rows(0)
    reduce_first(5)
    reduce_second(4)
    grads(0, 1)
    reduce_second(5)
    grads(1, 1)
    finish(1)
    gather_first(4)
    gather_second(3)
    send_grads(7)
    own_rows()
    return_rows(0)
    send_grads(6)
    gather_first(5)
    send_partner_rows(1)
    finish(3)
    gather_second(4)
    finish(2)
    finish(0)
    reduce_first(7)
    reduce_first(6)
    reduce_second(7)
    reduce_second(6)
    return_rows(1)
    gather_first(7)
    gather_first(6)
    combine(0)
    along_z(0)
    gather_second(6)
    finish(4)
    gather_second(5)
    gather_second(7)
    combine(1)
    along_z(1)
    tokens_out(0)
    finish(7)
    finish(5)
    finish(6)
    tokens_out(1)
    for c in done:
        c.wait()
    for c in pending.values():
        c.wait_send()


SCRATCH = (
    ((GN - 1, 8, GT), F32),
    ((2, GT, D), BF16),
    ((ROWS, GT), BF16),
    ((ROWS, 128), F32),
    ((2, XN - 1, CHUNK, D), BF16),
    ((2, 2 * ROWS, D), BF16),
    ((3 * HALF, D), BF16),
    ((2 * ROWS, 2 * HALF), F32),
    ((2 * ROWS, HALF), F32),
    ((2 * ROWS, 2 * HALF), BF16),
    ((6 * BLK, 2 * ROWS), BF16),
    ((3, BLK, D), F32),
    ((3, BLK, D), BF16),
    ((3, BLK, D), BF16),
    ((8, QUART, D // 4), BF16),
    ((8, QUART, D // 4), BF16),
    ((8, QUART, D // 2), BF16),
    ((8, QUART, D // 2), BF16),
    ((3, BLK, D), BF16),
    ((ROWS, D), F32),
    ((ROWS, D), BF16),
    ((ROWS, D), BF16),
    ((ROWS, D), BF16),
    ((GT, D), BF16),
    ((2 * TOK, D), BF16),
    ((TOK, D), BF16),
    ((TOK, D), BF16),
    ((TOK, D), BF16),
)


def local(inputs, upstream, gates, routes, w_gate, w_up, w_down):
    meta = jnp.concatenate(
        [routes.T.astype(F32), gates.T, jnp.zeros((4, TOK), F32)], axis=0
    )
    meta = jnp.tile(meta, (1, GN))
    anywhere = pl.BlockSpec(memory_space=pl.ANY)
    outs = pl.pallas_call(
        kernel,
        out_shape=(
            jax.ShapeDtypeStruct((TOK, D), BF16),
            jax.ShapeDtypeStruct((BLK, D), BF16),
            jax.ShapeDtypeStruct((BLK, D), BF16),
            jax.ShapeDtypeStruct((BLK, D), BF16),
        ),
        in_specs=[pl.BlockSpec(memory_space=pltpu.VMEM)] + [anywhere] * 5,
        out_specs=[anywhere] * 4,
        scratch_shapes=[pltpu.VMEM(shape, dtype) for shape, dtype in SCRATCH]
        + [
            pltpu.SemaphoreType.DMA((NSEM,)),
            pltpu.SemaphoreType.DMA((NSEM,)),
            pltpu.SemaphoreType.DMA((16,)),
        ],
        compiler_params=pltpu.CompilerParams(
            collective_id=0, has_side_effects=True, vmem_limit_bytes=62 * 2**20
        ),
        name="expert_backward",
    )(meta, inputs, upstream, w_gate[0], w_up[0], w_down[0])
    return outs[0], outs[1][None], outs[2][None], outs[3][None]


def solution(mesh):
    tokens = P(("expert", "fsdp", "dp"), None)
    hidden = P("expert", "fsdp", None)
    return jax.shard_map(
        local,
        mesh=mesh,
        in_specs=(tokens, tokens, tokens, tokens, hidden, hidden, hidden),
        out_specs=(tokens, hidden, hidden, hidden),
        check_vma=False,
    )
```

```python
import functools

import jax
import jax.numpy as jnp
from jax import lax
from jax.experimental import pallas as pl
from jax.experimental.pallas import tpu as pltpu
from jax.sharding import PartitionSpec as P

MESH_ID = pl.DeviceIdType.MESH
F32 = jnp.float32
BF16 = jnp.bfloat16

TOK = 96
CAP = 36
D = 2048
BLK = 192
XN = 4
GN = 4
FN = 4
DN = 4
GT = GN * TOK
CHUNK = GN * CAP
ROWS = XN * CHUNK
HALF = 2 * BLK
QUART = BLK // DN
NC = 4
CUTS = ((0, 256, 768, 1280, 2048), (0, 768, 1280, 1792, 2048))

NSEM = 192
SPREAD = (2,)


def chunk(a, c):
    return pl.ds(CUTS[a][c], CUTS[a][c + 1] - CUTS[a][c])


def dot_nt(a, b):
    return lax.dot_general(a, b, (((1,), (1,)), ((), ())), preferred_element_type=F32)


def dot_nn(a, b):
    return lax.dot_general(a, b, (((1,), (0,)), ((), ())), preferred_element_type=F32)


def dot_tn(a, b):
    return lax.dot_general(a, b, (((0,), (0,)), ((), ())), preferred_element_type=F32)


def kernel(
    meta_ref, x_ref, u_ref, wg_ref, wu_ref, wd_ref,
    out_x, out_g, out_u, out_d,
    metas, tok, tab, gsl, snd, rows, wts, gu, dh, dgu, tr, gacc, gsend, grecv,
    red_a, red_b, red_p, red_n, fin, p_own, p_send, p_recv, q, part, core_recv,
    z_send, z_recv, gout, ssem, rsem, lsem,
):
    e = lax.axis_index("expert")
    f = lax.axis_index("fsdp")
    d = lax.axis_index("dp")
    core = lax.rem(e, 2)
    sib_e = e + 1 - 2 * core
    zp_e = e + 2 - 4 * lax.rem(lax.div(e, 2), 2)
    diag_e = zp_e + 1 - 2 * core
    near = f + 1 - 2 * lax.rem(f, 2)
    far = FN - 1 - f
    row_f = near + core * (far - near)
    wgt_f = far + core * (near - far)
    up_d = lax.rem(d + 1, DN)
    dn_d = lax.rem(d + DN - 1, DN)
    op_d = lax.rem(d + 2, DN)

    sib = {"expert": sib_e}
    zp = {"expert": zp_e}
    diag = {"expert": diag_e}
    x_at = [{"expert": lax.rem(e + GN * o, XN * GN)} for o in range(XN)]
    row_y = {"fsdp": row_f}
    wgt_y = {"fsdp": wgt_f}
    d_up = {"dp": up_d}
    d_dn = {"dp": dn_d}

    used = [0]

    def remote(src, dst, dev):
        i = used[0]
        used[0] += 1
        return pltpu.make_async_remote_copy(
            src_ref=src, dst_ref=dst, send_sem=ssem.at[i], recv_sem=rsem.at[i],
            device_id=dev, device_id_type=MESH_ID,
        )

    pending = {}

    def send(src, dst, dev):
        c = remote(src, dst, dev)
        c.start()
        pending[id(c)] = c
        return c

    lused = [0]

    def local_copy(src, dst):
        i = lused[0]
        lused[0] += 1
        c = pltpu.make_async_copy(src, dst, lsem.at[i])
        c.start()
        return c

    toks = (x_ref, u_ref)
    own_tok = [local_copy(toks[a], tok.at[a, pl.ds(0, TOK)]) for a in range(2)]
    weights = (wg_ref, wu_ref, wd_ref)
    own_wts = [local_copy(weights[m], wts.at[pl.ds(m * HALF, BLK)]) for m in range(3)]

    partners = [sib, zp, diag] + x_at[1:] + [row_y, wgt_y, d_up, d_dn]
    barrier = pltpu.get_barrier_semaphore()
    for dev in partners:
        pl.semaphore_signal(barrier, inc=1, device_id=dev, device_id_type=MESH_ID)
    pl.semaphore_wait(barrier, len(partners))

    def quarter(i):
        return pl.ds(pl.multiple_of(i * QUART, QUART), QUART)

    def wts_quarter(m, i):
        return pl.ds(pl.multiple_of(m * HALF + BLK + i * QUART, QUART), QUART)

    meta_c = [send(meta_ref, metas.at[i], dev) for i, dev in enumerate((zp, sib, diag))]
    tok_z = {}
    tok_s = {}

    def send_tokens(a, c):
        cols = chunk(a, c)
        mine = tok.at[a, pl.ds(0, TOK), cols]
        tok_z[a, c] = send(mine, tok.at[a, pl.ds(TOK, TOK), cols], zp)
        tok_s[a, c] = send(mine, tok.at[a, pl.ds(2 * TOK, TOK), cols], sib)

    steps = [(a, c) for a in range(2) for c in range(NC)]
    own_tok[0].wait()
    for step in steps[:2]:
        send_tokens(*step)
    own_tok[1].wait()
    w_y = {}
    for m in range(3):
        own_wts[m].wait()
        if m in SPREAD:
            src = wts.at[pl.ds(pl.multiple_of(m * HALF + d * QUART, QUART), QUART), :]
            w_y[m] = send(src, wts.at[wts_quarter(m, d), :], wgt_y)
        else:
            src = wts.at[pl.ds(m * HALF, BLK)]
            w_y[m] = send(src, wts.at[pl.ds(m * HALF + BLK, BLK)], wgt_y)
    w1 = {}
    w2 = {}
    lo = pl.ds(0, D // 2)
    hi = pl.ds(D // 2, D // 2)

    def weights_first(m):
        w_y[m].wait_recv()
        at = wts_quarter(m, d)
        w1[m] = (
            send(wts.at[at, :], wts.at[at, :], d_up),
            send(wts.at[at, :], wts.at[at, :], d_dn),
        )

    def weights_second(m):
        w1[m][0].wait_recv()
        at = wts_quarter(m, dn_d)
        first_c = send(wts.at[at, lo], wts.at[at, lo], d_up)
        w1[m][1].wait_recv()
        at = wts_quarter(m, up_d)
        w2[m] = (first_c, send(wts.at[at, hi], wts.at[at, hi], d_dn))

    for c in meta_c:
        c.wait_recv()
    lane = lax.broadcasted_iota(jnp.int32, (8, GT), 1)
    meta = meta_ref[...]
    for r in range(1, GN):
        meta = jnp.where(lane >= r * TOK, metas[r - 1], meta)
    source = sum((lane >= r * TOK).astype(F32) for r in range(1, GN))
    relative = lax.broadcasted_iota(jnp.int32, (8, GT), 0)
    expert = lax.rem(e + GN * relative, XN * GN).astype(F32)
    hit0 = meta[0:1] == expert
    hit1 = meta[1:2] == expert
    hit = jnp.logical_or(hit0, hit1)
    t_row = lax.broadcasted_iota(jnp.int32, (GT, GT), 0)
    t_col = lax.broadcasted_iota(jnp.int32, (GT, GT), 1)
    first = sum(jnp.where(t_col >= r * TOK, TOK, 0) for r in range(1, GN))
    before = jnp.logical_and(t_row < t_col, t_row >= first)
    earlier = dot_nn(
        jnp.where(hit, 1.0, 0.0).astype(BF16), jnp.where(before, 1.0, 0.0).astype(BF16)
    )
    target = jnp.where(hit, source * CAP + earlier, -1.0)
    weight = jnp.where(hit0, meta[2:3], jnp.where(hit1, meta[3:4], 0.0))
    slot = lax.broadcasted_iota(jnp.int32, (CHUNK, GT), 0).astype(F32)
    for o in range(XN):
        same = slot == target[o : o + 1]
        at = pl.ds(o * CHUNK, CHUNK)
        tab[at, :] = jnp.where(same, 1.0, 0.0).astype(BF16)
        gates = jnp.sum(jnp.where(same, weight[o : o + 1], 0.0), axis=1, keepdims=True)
        gsl[at, :] = jnp.broadcast_to(gates, (CHUNK, 128))

    x_c = {}
    y_c = {}

    def pick(a, c):
        cols = chunk(a, c)
        picked = dot_nn(tab[...], tok[a, :, cols])
        if a == 1:
            picked = picked * gsl[:, 0:1]
        picked = picked.astype(BF16)
        rows[a, pl.ds(0, CHUNK), cols] = picked[0:CHUNK]
        for o in range(1, XN):
            snd[a, o - 1, :, cols] = picked[o * CHUNK : (o + 1) * CHUNK]

    def send_rows(a, c):
        cols = chunk(a, c)
        for o in (2, 1, 3):
            x_c[a, c, o] = send(
                snd.at[a, o - 1, :, cols],
                rows.at[a, pl.ds((XN - o) * CHUNK, CHUNK), cols],
                x_at[o],
            )

    def pass_on(a, c):
        for o in (1, 3, 2):
            x_c[a, c, o].wait_recv()
        cols = chunk(a, c)
        y_c[a, c] = send(
            rows.at[a, pl.ds(0, ROWS), cols], rows.at[a, pl.ds(ROWS, ROWS), cols], row_y
        )

    def gate_up(s):
        at = pl.ds(s * ROWS, ROWS)

        @pl.loop(0, 3)
        def _(n):
            tile = pl.ds(pl.multiple_of(n * 256, 256), 256)
            gu[at, tile] = dot_nt(rows[0, at, :], wts[tile, :])

    def d_hidden(s):
        if s == 1:
            for c in range(NC):
                need(c)
        at = pl.ds(s * ROWS, ROWS)
        dh[at, :] = dot_nt(rows[1, at, :], wts[pl.ds(2 * HALF, HALF), :])

    def turn(m, at, value):
        turned = value.T
        tr[pl.ds(m * BLK, BLK), at] = turned[BLK:HALF]
        tr[pl.ds((3 + m) * BLK, BLK), at] = turned[0:BLK]

    def make_hidden():
        @pl.loop(0, 2 * ROWS // 128)
        def _(i):
            at = pl.ds(pl.multiple_of(i * 128, 128), 128)
            gate = gu[at, pl.ds(0, HALF)]
            upward = gu[at, pl.ds(HALF, HALF)]
            logistic = jax.nn.sigmoid(gate)
            active = gate * logistic
            slope = logistic * (1.0 + gate * (1.0 - logistic))
            gu[at, pl.ds(0, HALF)] = upward * slope
            gu[at, pl.ds(HALF, HALF)] = active
            turn(2, at, (active * upward).astype(BF16))

    def elementwise(low, high):
        @pl.loop(low, high)
        def _(i):
            at = pl.ds(pl.multiple_of(i * 128, 128), 128)
            dhid = dh[at, :]
            for m in range(2):
                cols = pl.ds(m * HALF, HALF)
                value = (dhid * gu[at, cols]).astype(BF16)
                dgu[at, cols] = value
                turn(m, at, value)

    def wait_weights(m):
        for c in w2[m] if m in SPREAD else (w_y[m],):
            c.wait_recv()

    for k, (a, c) in enumerate(steps):
        if k + 2 < len(steps):
            send_tokens(*steps[k + 2])
        cols = chunk(a, c)
        tok_z[a, c].wait_recv()
        fwd = send(tok.at[a, pl.ds(TOK, TOK), cols], tok.at[a, pl.ds(3 * TOK, TOK), cols], sib)
        tok_s[a, c].wait_recv()
        fwd.wait_recv()
        pick(a, c)
        send_rows(a, c)
        if k >= 2:
            pass_on(*steps[k - 2])
        for m in SPREAD:
            if k == 2 + m:
                weights_first(m)
            if k == 5 + m:
                weights_second(m)
        if k == NC + 2:
            for m in range(2):
                wait_weights(m)
            gate_up(0)
        if k == NC + 3:
            for i in range(NC):
                y_c[0, i].wait_recv()
            gate_up(1)

    parts = [(2, CUTS[1][c], CUTS[1][c + 1] - CUTS[1][c]) for c in range(NC)]
    half_d = D // 2
    parts += [(m, h * half_d, half_d) for h in range(2) for m in range(2)]

    landed = set()

    def need(c):
        if c not in landed:
            y_c[1, c].wait_recv()
            landed.add(c)

    def grads_down(c):
        need(c)
        cols = chunk(1, c)
        gsend[2, :, cols] = dot_nn(tr[pl.ds(2 * BLK, BLK), :], rows[1, :, cols]).astype(BF16)
        send_grads(c)
        gacc[2, :, cols] = dot_nn(tr[pl.ds(5 * BLK, BLK), :], rows[1, :, cols])

    def grads(mine, h):
        @pl.loop(0, half_d // 512)
        def _(n):
            tile = pl.ds(pl.multiple_of(h * half_d + n * 512, 512), 512)
            value = dot_nn(tr[pl.ds(3 * BLK * mine, 2 * BLK), :], rows[0, :, tile])
            for i in range(2):
                one = value[i * BLK : (i + 1) * BLK]
                if mine:
                    gacc[i, :, tile] = one
                else:
                    gsend[i, :, tile] = one.astype(BF16)

    g_c = {}

    def send_grads(j):
        m, low, width = parts[j]
        cols = pl.ds(low, width)
        g_c[j] = send(gsend.at[m, :, cols], grecv.at[m, :, cols], wgt_y)

    p_c = {}

    def partner_rows(c):
        @pl.loop(0, half_d // 512)
        def _(n):
            tile = pl.ds(pl.multiple_of(c * half_d + n * 512, 512), 512)
            p_send[:, tile] = dot_nn(
                dgu[pl.ds(ROWS, ROWS), :], wts[pl.ds(0, 2 * HALF), tile]
            ).astype(BF16)

    def send_partner_rows(c):
        cols = pl.ds(c * half_d, half_d)
        p_c[c] = send(p_send.at[:, cols], p_recv.at[:, cols], row_y)

    r1 = {}
    r2 = {}
    a1 = {}
    a2 = {}

    def split(j):
        m, low, width = parts[j]
        half = width // 2
        return (
            m, pl.ds(low, half), pl.ds(low + half, half), pl.ds(low, width),
            pl.ds(0, half), pl.ds(0, width),
        )

    def reduce_first(j):
        m, low, high, cols, narrow, wide = split(j)
        g_c[j].wait_recv()
        g_c[j].wait_send()
        del pending[id(g_c[j])]

        @pl.loop(0, BLK // 16)
        def _(i):
            at = pl.ds(pl.multiple_of(i * 16, 16), 16)
            gsend[m, at, cols] = (
                gacc[m, at, cols] + grecv[m, at, cols].astype(F32)
            ).astype(BF16)

        r1[j] = (
            send(gsend.at[m, quarter(op_d), low], red_a.at[j, :, narrow], d_up),
            send(gsend.at[m, quarter(op_d), high], red_b.at[j, :, narrow], d_dn),
        )

    def reduce_second(j):
        m, low, high, cols, narrow, wide = split(j)
        r1[j][0].wait_recv()
        at = quarter(up_d)
        gsend[m, at, low] = (gsend[m, at, low].astype(F32) + red_a[j, :, narrow].astype(F32)).astype(BF16)
        first_c = send(gsend.at[m, at, cols], red_p.at[j, :, wide], d_up)
        r1[j][1].wait_recv()
        at = quarter(dn_d)
        gsend[m, at, high] = (gsend[m, at, high].astype(F32) + red_b[j, :, narrow].astype(F32)).astype(BF16)
        r2[j] = (first_c, send(gsend.at[m, at, cols], red_n.at[j, :, wide], d_dn))

    def gather_first(j):
        m, low, high, cols, narrow, wide = split(j)
        r2[j][0].wait_recv()
        r2[j][1].wait_recv()
        at = quarter(d)
        fin[m, at, cols] = (
            gsend[m, at, cols].astype(F32) + red_p[j, :, wide].astype(F32) + red_n[j, :, wide].astype(F32)
        ).astype(BF16)
        a1[j] = (
            send(fin.at[m, at, cols], fin.at[m, at, cols], d_up),
            send(fin.at[m, at, cols], fin.at[m, at, cols], d_dn),
        )

    def gather_second(j):
        m, low, high, cols, narrow, wide = split(j)
        a1[j][0].wait_recv()
        at = quarter(dn_d)
        first_c = send(fin.at[m, at, low], fin.at[m, at, low], d_up)
        a1[j][1].wait_recv()
        at = quarter(up_d)
        a2[j] = (first_c, send(fin.at[m, at, high], fin.at[m, at, high], d_dn))

    outs = (out_g, out_u, out_d)
    done = []

    def finish(j):
        m, low, high, cols, narrow, wide = split(j)
        a2[j][0].wait_recv()
        a2[j][1].wait_recv()
        done.append(local_copy(fin.at[m, :, cols], outs[m].at[:, cols]))

    q_c = {}
    s_c = {}
    z_c = {}

    def own_rows():
        @pl.loop(0, D // 512)
        def _(n):
            tile = pl.ds(pl.multiple_of(n * 512, 512), 512)
            p_own[:, tile] = dot_nn(dgu[pl.ds(0, ROWS), :], wts[pl.ds(0, 2 * HALF), tile])

    def return_rows(c):
        cols = pl.ds(c * half_d, half_d)
        p_c[c].wait_recv()
        p_c[c].wait_send()
        del pending[id(p_c[c])]

        @pl.loop(0, ROWS // 48)
        def _(i):
            at = pl.ds(pl.multiple_of(i * 48, 48), 48)
            p_send[at, cols] = (p_own[at, cols] + p_recv[at, cols].astype(F32)).astype(BF16)

        for k in (2, 1, 3):
            q_c[c, k] = send(
                p_send.at[pl.ds(k * CHUNK, CHUNK), cols],
                q.at[pl.ds((XN - k) * CHUNK, CHUNK), cols],
                x_at[k],
            )
        q[pl.ds(0, CHUNK), cols] = p_send[pl.ds(0, CHUNK), cols]

    def combine(c):
        cols = pl.ds(c * half_d, half_d)
        for k in (1, 3, 2):
            q_c[c, k].wait_recv()

        @pl.loop(0, half_d // 512)
        def _(n):
            tile = pl.ds(pl.multiple_of(c * half_d + n * 512, 512), 512)
            part[:, tile] = dot_tn(tab[...], q[:, tile]).astype(BF16)

        s_c[c] = send(part.at[pl.ds(2 * TOK, 2 * TOK), cols], core_recv.at[:, cols], sib)

    def along_z(c):
        cols = pl.ds(c * half_d, half_d)
        s_c[c].wait_recv()
        z_send[:, cols] = (
            part[pl.ds(TOK, TOK), cols].astype(F32)
            + core_recv[pl.ds(TOK, TOK), cols].astype(F32)
        ).astype(BF16)
        z_c[c] = send(z_send.at[:, cols], z_recv.at[:, cols], zp)

    def tokens_out(c):
        cols = pl.ds(c * half_d, half_d)
        z_c[c].wait_recv()
        gout[:, cols] = (
            part[pl.ds(0, TOK), cols].astype(F32)
            + core_recv[pl.ds(0, TOK), cols].astype(F32)
            + z_recv[:, cols].astype(F32)
        ).astype(BF16)
        done.append(local_copy(gout.at[:, cols], out_x.at[:, cols]))

    wait_weights(2)
    make_hidden()
    grads_down(0)
    grads_down(1)
    pass_on(*steps[-2])
    reduce_first(0)
    reduce_first(1)
    reduce_second(0)
    pass_on(*steps[-1])
    d_hidden(0)
    elementwise(0, ROWS // 128)
    reduce_second(1)
    grads_down(2)
    gather_first(0)
    d_hidden(1)
    elementwise(ROWS // 128, 2 * ROWS // 128)
    gather_first(1)
    grads_down(3)
    grads(0, 0)
    send_grads(4)
    reduce_first(2)
    partner_rows(1)
    gather_second(0)
    reduce_first(3)
    grads(1, 0)
    send_grads(5)
    reduce_second(2)
    grads(0, 1)
    reduce_second(3)
    grads(1, 1)
    reduce_first(4)
    partner_rows(0)
    send_grads(7)
    gather_second(1)
    reduce_first(5)
    send_grads(6)
    reduce_second(4)
    gather_first(3)
    reduce_first(7)
    send_partner_rows(0)
    gather_first(2)
    reduce_second(5)
    own_rows()
    gather_first(4)
    reduce_second(7)
    finish(1)
    reduce_first(6)
    send_partner_rows(1)
    gather_first(5)
    return_rows(0)
    gather_second(2)
    gather_second(3)
    return_rows(1)
    reduce_second(6)
    gather_first(7)
    gather_second(5)
    gather_second(4)
    combine(0)
    along_z(0)
    gather_first(6)
    finish(2)
    finish(5)
    finish(4)
    combine(1)
    gather_second(7)
    along_z(1)
    tokens_out(0)
    finish(3)
    finish(7)
    finish(0)
    gather_second(6)
    tokens_out(1)
    finish(6)
    for c in done:
        c.wait()
    for c in pending.values():
        c.wait_send()


SCRATCH = (
    ((GN - 1, 8, GT), F32),
    ((2, GT, D), BF16),
    ((ROWS, GT), BF16),
    ((ROWS, 128), F32),
    ((2, XN - 1, CHUNK, D), BF16),
    ((2, 2 * ROWS, D), BF16),
    ((3 * HALF, D), BF16),
    ((2 * ROWS, 2 * HALF), F32),
    ((2 * ROWS, HALF), F32),
    ((2 * ROWS, 2 * HALF), BF16),
    ((6 * BLK, 2 * ROWS), BF16),
    ((3, BLK, D), F32),
    ((3, BLK, D), BF16),
    ((3, BLK, D), BF16),
    ((8, QUART, D // 4), BF16),
    ((8, QUART, D // 4), BF16),
    ((8, QUART, D // 2), BF16),
    ((8, QUART, D // 2), BF16),
    ((3, BLK, D), BF16),
    ((ROWS, D), F32),
    ((ROWS, D), BF16),
    ((ROWS, D), BF16),
    ((ROWS, D), BF16),
    ((GT, D), BF16),
    ((2 * TOK, D), BF16),
    ((TOK, D), BF16),
    ((TOK, D), BF16),
    ((TOK, D), BF16),
)


def local(inputs, upstream, gates, routes, w_gate, w_up, w_down):
    meta = jnp.concatenate(
        [routes.T.astype(F32), gates.T, jnp.zeros((4, TOK), F32)], axis=0
    )
    meta = jnp.tile(meta, (1, GN))
    anywhere = pl.BlockSpec(memory_space=pl.ANY)
    outs = pl.pallas_call(
        kernel,
        out_shape=(
            jax.ShapeDtypeStruct((TOK, D), BF16),
            jax.ShapeDtypeStruct((BLK, D), BF16),
            jax.ShapeDtypeStruct((BLK, D), BF16),
            jax.ShapeDtypeStruct((BLK, D), BF16),
        ),
        in_specs=[pl.BlockSpec(memory_space=pltpu.VMEM)] + [anywhere] * 5,
        out_specs=[anywhere] * 4,
        scratch_shapes=[pltpu.VMEM(shape, dtype) for shape, dtype in SCRATCH]
        + [
            pltpu.SemaphoreType.DMA((NSEM,)),
            pltpu.SemaphoreType.DMA((NSEM,)),
            pltpu.SemaphoreType.DMA((16,)),
        ],
        compiler_params=pltpu.CompilerParams(
            collective_id=0, has_side_effects=True, vmem_limit_bytes=62 * 2**20
        ),
        name="expert_backward",
    )(meta, inputs, upstream, w_gate[0], w_up[0], w_down[0])
    return outs[0], outs[1][None], outs[2][None], outs[3][None]


def solution(mesh):
    tokens = P(("expert", "fsdp", "dp"), None)
    hidden = P("expert", "fsdp", None)
    return jax.shard_map(
        local,
        mesh=mesh,
        in_specs=(tokens, tokens, tokens, tokens, hidden, hidden, hidden),
        out_specs=(tokens, hidden, hidden, hidden),
        check_vma=False,
    )
```

```python
import functools

import jax
import jax.numpy as jnp
from jax import lax
from jax.experimental import pallas as pl
from jax.experimental.pallas import tpu as pltpu
from jax.sharding import PartitionSpec as P

MESH_ID = pl.DeviceIdType.MESH
F32 = jnp.float32
BF16 = jnp.bfloat16

TOK = 96
CAP = 36
D = 2048
BLK = 192
XN = 4
GN = 4
FN = 4
DN = 4
GT = GN * TOK
CHUNK = GN * CAP
ROWS = XN * CHUNK
HALF = 2 * BLK
QUART = BLK // DN
NC = 4
CUTS = ((0, 256, 768, 1280, 2048), (0, 768, 1280, 1792, 2048))

NSEM = 224
SPREAD = (2,)


def chunk(a, c):
    return pl.ds(CUTS[a][c], CUTS[a][c + 1] - CUTS[a][c])


def dot_nt(a, b):
    return lax.dot_general(a, b, (((1,), (1,)), ((), ())), preferred_element_type=F32)


def dot_nn(a, b):
    return lax.dot_general(a, b, (((1,), (0,)), ((), ())), preferred_element_type=F32)


def dot_tn(a, b):
    return lax.dot_general(a, b, (((0,), (0,)), ((), ())), preferred_element_type=F32)


def kernel(
    meta_ref, x_ref, u_ref, wg_ref, wu_ref, wd_ref,
    out_x, out_g, out_u, out_d,
    metas, tok, tab, gsl, snd, rows, wts, gu, dh, dgu, tr, gacc, gsend, grecv,
    red_a, red_b, red_p, red_n, fin, p_own, p_send, p_recv, q, part, core_recv,
    z_send, z_recv, gout, ssem, rsem, lsem,
):
    e = lax.axis_index("expert")
    f = lax.axis_index("fsdp")
    d = lax.axis_index("dp")
    core = lax.rem(e, 2)
    sib_e = e + 1 - 2 * core
    zp_e = e + 2 - 4 * lax.rem(lax.div(e, 2), 2)
    diag_e = zp_e + 1 - 2 * core
    near = f + 1 - 2 * lax.rem(f, 2)
    far = FN - 1 - f
    row_f = near + core * (far - near)
    wgt_f = far + core * (near - far)
    up_d = lax.rem(d + 1, DN)
    dn_d = lax.rem(d + DN - 1, DN)
    op_d = lax.rem(d + 2, DN)

    sib = {"expert": sib_e}
    zp = {"expert": zp_e}
    diag = {"expert": diag_e}
    x_at = [{"expert": lax.rem(e + GN * o, XN * GN)} for o in range(XN)]
    row_y = {"fsdp": row_f}
    wgt_y = {"fsdp": wgt_f}
    d_up = {"dp": up_d}
    d_dn = {"dp": dn_d}

    used = [0]

    def remote(src, dst, dev):
        i = used[0]
        used[0] += 1
        return pltpu.make_async_remote_copy(
            src_ref=src, dst_ref=dst, send_sem=ssem.at[i], recv_sem=rsem.at[i],
            device_id=dev, device_id_type=MESH_ID,
        )

    pending = {}

    def send(src, dst, dev):
        c = remote(src, dst, dev)
        c.start()
        pending[id(c)] = c
        return c

    lused = [0]

    def local_copy(src, dst):
        i = lused[0]
        lused[0] += 1
        c = pltpu.make_async_copy(src, dst, lsem.at[i])
        c.start()
        return c

    toks = (x_ref, u_ref)
    own_tok = [local_copy(toks[a], tok.at[a, pl.ds(0, TOK)]) for a in range(2)]
    weights = (wg_ref, wu_ref, wd_ref)
    own_wts = [local_copy(weights[m], wts.at[pl.ds(m * HALF, BLK)]) for m in range(3)]

    partners = [sib, zp, diag] + x_at[1:] + [row_y, wgt_y, d_up, d_dn]
    barrier = pltpu.get_barrier_semaphore()
    for dev in partners:
        pl.semaphore_signal(barrier, inc=1, device_id=dev, device_id_type=MESH_ID)
    pl.semaphore_wait(barrier, len(partners))

    def quarter(i):
        return pl.ds(pl.multiple_of(i * QUART, QUART), QUART)

    def wts_quarter(m, i):
        return pl.ds(pl.multiple_of(m * HALF + BLK + i * QUART, QUART), QUART)

    meta_c = [send(meta_ref, metas.at[i], dev) for i, dev in enumerate((zp, sib, diag))]
    tok_z = {}
    tok_s = {}

    def send_tokens(a, c):
        cols = chunk(a, c)
        mine = tok.at[a, pl.ds(0, TOK), cols]
        tok_z[a, c] = send(mine, tok.at[a, pl.ds(TOK, TOK), cols], zp)
        tok_s[a, c] = send(mine, tok.at[a, pl.ds(2 * TOK, TOK), cols], sib)

    steps = [(a, c) for a in range(2) for c in range(NC)]
    own_tok[0].wait()
    for step in steps[:2]:
        send_tokens(*step)
    own_tok[1].wait()
    w_y = {}
    for m in range(3):
        own_wts[m].wait()
        if m in SPREAD:
            src = wts.at[pl.ds(pl.multiple_of(m * HALF + d * QUART, QUART), QUART), :]
            w_y[m] = send(src, wts.at[wts_quarter(m, d), :], wgt_y)
        else:
            src = wts.at[pl.ds(m * HALF, BLK)]
            w_y[m] = send(src, wts.at[pl.ds(m * HALF + BLK, BLK)], wgt_y)
    w1 = {}
    w2 = {}
    lo = pl.ds(0, D // 2)
    hi = pl.ds(D // 2, D // 2)

    def weights_first(m):
        w_y[m].wait_recv()
        at = wts_quarter(m, d)
        w1[m] = (
            send(wts.at[at, :], wts.at[at, :], d_up),
            send(wts.at[at, :], wts.at[at, :], d_dn),
        )

    def weights_second(m):
        w1[m][0].wait_recv()
        at = wts_quarter(m, dn_d)
        first_c = send(wts.at[at, lo], wts.at[at, lo], d_up)
        w1[m][1].wait_recv()
        at = wts_quarter(m, up_d)
        w2[m] = (first_c, send(wts.at[at, hi], wts.at[at, hi], d_dn))

    for c in meta_c:
        c.wait_recv()
    lane = lax.broadcasted_iota(jnp.int32, (8, GT), 1)
    meta = meta_ref[...]
    for r in range(1, GN):
        meta = jnp.where(lane >= r * TOK, metas[r - 1], meta)
    source = sum((lane >= r * TOK).astype(F32) for r in range(1, GN))
    relative = lax.broadcasted_iota(jnp.int32, (8, GT), 0)
    expert = lax.rem(e + GN * relative, XN * GN).astype(F32)
    hit0 = meta[0:1] == expert
    hit1 = meta[1:2] == expert
    hit = jnp.logical_or(hit0, hit1)
    t_row = lax.broadcasted_iota(jnp.int32, (GT, GT), 0)
    t_col = lax.broadcasted_iota(jnp.int32, (GT, GT), 1)
    first = sum(jnp.where(t_col >= r * TOK, TOK, 0) for r in range(1, GN))
    before = jnp.logical_and(t_row < t_col, t_row >= first)
    earlier = dot_nn(
        jnp.where(hit, 1.0, 0.0).astype(BF16), jnp.where(before, 1.0, 0.0).astype(BF16)
    )
    target = jnp.where(hit, source * CAP + earlier, -1.0)
    weight = jnp.where(hit0, meta[2:3], jnp.where(hit1, meta[3:4], 0.0))
    slot = lax.broadcasted_iota(jnp.int32, (CHUNK, GT), 0).astype(F32)
    for o in range(XN):
        same = slot == target[o : o + 1]
        at = pl.ds(o * CHUNK, CHUNK)
        tab[at, :] = jnp.where(same, 1.0, 0.0).astype(BF16)
        gates = jnp.sum(jnp.where(same, weight[o : o + 1], 0.0), axis=1, keepdims=True)
        gsl[at, :] = jnp.broadcast_to(gates, (CHUNK, 128))

    x_c = {}
    y_c = {}

    def pick(a, c):
        cols = chunk(a, c)
        picked = dot_nn(tab[...], tok[a, :, cols])
        if a == 1:
            picked = picked * gsl[:, 0:1]
        picked = picked.astype(BF16)
        rows[a, pl.ds(0, CHUNK), cols] = picked[0:CHUNK]
        for o in range(1, XN):
            snd[a, o - 1, :, cols] = picked[o * CHUNK : (o + 1) * CHUNK]

    def send_rows(a, c):
        cols = chunk(a, c)
        for o in (2, 1, 3):
            x_c[a, c, o] = send(
                snd.at[a, o - 1, :, cols],
                rows.at[a, pl.ds((XN - o) * CHUNK, CHUNK), cols],
                x_at[o],
            )

    def pass_on(a, c):
        for o in (1, 3, 2):
            x_c[a, c, o].wait_recv()
        cols = chunk(a, c)
        y_c[a, c] = send(
            rows.at[a, pl.ds(0, ROWS), cols], rows.at[a, pl.ds(ROWS, ROWS), cols], row_y
        )

    def gate_up(s):
        at = pl.ds(s * ROWS, ROWS)
        if s == 0:
            wait_weights(0)
            wait_weights(1)
        else:
            for c in range(NC):
                y_c[0, c].wait_recv()

        @pl.loop(0, 3)
        def _(n):
            tile = pl.ds(pl.multiple_of(n * 256, 256), 256)
            gu[at, tile] = dot_nt(rows[0, at, :], wts[tile, :])

    def d_hidden(s):
        if s == 0:
            wait_weights(2)
        else:
            for c in range(NC):
                need(c)
        at = pl.ds(s * ROWS, ROWS)
        dh[at, :] = dot_nt(rows[1, at, :], wts[pl.ds(2 * HALF, HALF), :])

    def turn(m, at, value):
        turned = value.T
        tr[pl.ds(m * BLK, BLK), at] = turned[BLK:HALF]
        tr[pl.ds((3 + m) * BLK, BLK), at] = turned[0:BLK]

    def make_hidden():
        @pl.loop(0, 2 * ROWS // 128)
        def _(i):
            at = pl.ds(pl.multiple_of(i * 128, 128), 128)
            gate = gu[at, pl.ds(0, HALF)]
            upward = gu[at, pl.ds(HALF, HALF)]
            logistic = jax.nn.sigmoid(gate)
            active = gate * logistic
            slope = logistic * (1.0 + gate * (1.0 - logistic))
            gu[at, pl.ds(0, HALF)] = upward * slope
            gu[at, pl.ds(HALF, HALF)] = active
            turn(2, at, (active * upward).astype(BF16))

    def elementwise(low, high):
        @pl.loop(low, high)
        def _(i):
            at = pl.ds(pl.multiple_of(i * 128, 128), 128)
            dhid = dh[at, :]
            for m in range(2):
                cols = pl.ds(m * HALF, HALF)
                value = (dhid * gu[at, cols]).astype(BF16)
                dgu[at, cols] = value
                turn(m, at, value)

    def wait_weights(m):
        for c in w2[m] if m in SPREAD else (w_y[m],):
            c.wait_recv()

    fwd = {}

    def forward(k):
        a, c = steps[k]
        cols = chunk(a, c)
        tok_z[a, c].wait_recv()
        fwd[k] = send(
            tok.at[a, pl.ds(TOK, TOK), cols], tok.at[a, pl.ds(3 * TOK, TOK), cols], sib
        )

    def front(k):
        a, c = steps[k]
        tok_s[a, c].wait_recv()
        fwd[k].wait_recv()
        pick(a, c)
        send_rows(a, c)


    parts = [(2, CUTS[1][c], CUTS[1][c + 1] - CUTS[1][c]) for c in range(NC)]
    half_d = D // 2
    parts += [(m, h * half_d, half_d) for h in range(2) for m in range(2)]

    landed = set()

    def need(c):
        if c not in landed:
            y_c[1, c].wait_recv()
            landed.add(c)

    def grads_down(c):
        need(c)
        cols = chunk(1, c)
        gsend[2, :, cols] = dot_nn(tr[pl.ds(2 * BLK, BLK), :], rows[1, :, cols]).astype(BF16)
        send_grads(c)
        gacc[2, :, cols] = dot_nn(tr[pl.ds(5 * BLK, BLK), :], rows[1, :, cols])

    def grads(mine, h):
        @pl.loop(0, half_d // 512)
        def _(n):
            tile = pl.ds(pl.multiple_of(h * half_d + n * 512, 512), 512)
            value = dot_nn(tr[pl.ds(3 * BLK * mine, 2 * BLK), :], rows[0, :, tile])
            for i in range(2):
                one = value[i * BLK : (i + 1) * BLK]
                if mine:
                    gacc[i, :, tile] = one
                else:
                    gsend[i, :, tile] = one.astype(BF16)

    g_c = {}

    def send_grads(j):
        m, low, width = parts[j]
        cols = pl.ds(low, width)
        g_c[j] = send(gsend.at[m, :, cols], grecv.at[m, :, cols], wgt_y)

    p_c = {}

    def partner_rows(c):
        @pl.loop(0, half_d // 512)
        def _(n):
            tile = pl.ds(pl.multiple_of(c * half_d + n * 512, 512), 512)
            p_send[:, tile] = dot_nn(
                dgu[pl.ds(ROWS, ROWS), :], wts[pl.ds(0, 2 * HALF), tile]
            ).astype(BF16)

    def send_partner_rows(c):
        cols = pl.ds(c * half_d, half_d)
        p_c[c] = send(p_send.at[:, cols], p_recv.at[:, cols], row_y)

    r1 = {}
    r2 = {}
    a1 = {}
    a2 = {}

    def split(j):
        m, low, width = parts[j]
        half = width // 2
        return (
            m, pl.ds(low, half), pl.ds(low + half, half), pl.ds(low, width),
            pl.ds(0, half), pl.ds(0, width),
        )

    def reduce_first(j):
        m, low, high, cols, narrow, wide = split(j)
        g_c[j].wait_recv()
        g_c[j].wait_send()
        del pending[id(g_c[j])]

        @pl.loop(0, BLK // 16)
        def _(i):
            at = pl.ds(pl.multiple_of(i * 16, 16), 16)
            gsend[m, at, cols] = (
                gacc[m, at, cols] + grecv[m, at, cols].astype(F32)
            ).astype(BF16)

        r1[j] = (
            send(gsend.at[m, quarter(op_d), low], red_a.at[j, :, narrow], d_up),
            send(gsend.at[m, quarter(op_d), high], red_b.at[j, :, narrow], d_dn),
        )

    def reduce_second(j):
        m, low, high, cols, narrow, wide = split(j)
        r1[j][0].wait_recv()
        at = quarter(up_d)
        gsend[m, at, low] = (gsend[m, at, low].astype(F32) + red_a[j, :, narrow].astype(F32)).astype(BF16)
        first_c = send(gsend.at[m, at, cols], red_p.at[j, :, wide], d_up)
        r1[j][1].wait_recv()
        at = quarter(dn_d)
        gsend[m, at, high] = (gsend[m, at, high].astype(F32) + red_b[j, :, narrow].astype(F32)).astype(BF16)
        r2[j] = (first_c, send(gsend.at[m, at, cols], red_n.at[j, :, wide], d_dn))

    def gather_first(j):
        m, low, high, cols, narrow, wide = split(j)
        r2[j][0].wait_recv()
        r2[j][1].wait_recv()
        at = quarter(d)
        fin[m, at, cols] = (
            gsend[m, at, cols].astype(F32) + red_p[j, :, wide].astype(F32) + red_n[j, :, wide].astype(F32)
        ).astype(BF16)
        a1[j] = (
            send(fin.at[m, at, cols], fin.at[m, at, cols], d_up),
            send(fin.at[m, at, cols], fin.at[m, at, cols], d_dn),
        )

    def gather_second(j):
        m, low, high, cols, narrow, wide = split(j)
        a1[j][0].wait_recv()
        at = quarter(dn_d)
        first_c = send(fin.at[m, at, low], fin.at[m, at, low], d_up)
        a1[j][1].wait_recv()
        at = quarter(up_d)
        a2[j] = (first_c, send(fin.at[m, at, high], fin.at[m, at, high], d_dn))

    outs = (out_g, out_u, out_d)
    done = []

    def finish(j):
        m, low, high, cols, narrow, wide = split(j)
        a2[j][0].wait_recv()
        a2[j][1].wait_recv()
        done.append(local_copy(fin.at[m, :, cols], outs[m].at[:, cols]))

    q_c = {}
    s_c = {}
    z_c = {}

    def own_rows():
        @pl.loop(0, D // 512)
        def _(n):
            tile = pl.ds(pl.multiple_of(n * 512, 512), 512)
            p_own[:, tile] = dot_nn(dgu[pl.ds(0, ROWS), :], wts[pl.ds(0, 2 * HALF), tile])

    def return_rows(c):
        cols = pl.ds(c * half_d, half_d)
        p_c[c].wait_recv()
        p_c[c].wait_send()
        del pending[id(p_c[c])]

        @pl.loop(0, ROWS // 48)
        def _(i):
            at = pl.ds(pl.multiple_of(i * 48, 48), 48)
            p_send[at, cols] = (p_own[at, cols] + p_recv[at, cols].astype(F32)).astype(BF16)

        for k in (2, 1, 3):
            q_c[c, k] = send(
                p_send.at[pl.ds(k * CHUNK, CHUNK), cols],
                q.at[pl.ds((XN - k) * CHUNK, CHUNK), cols],
                x_at[k],
            )
        q[pl.ds(0, CHUNK), cols] = p_send[pl.ds(0, CHUNK), cols]

    def combine(c):
        cols = pl.ds(c * half_d, half_d)
        for k in (1, 3, 2):
            q_c[c, k].wait_recv()

        @pl.loop(0, half_d // 512)
        def _(n):
            tile = pl.ds(pl.multiple_of(c * half_d + n * 512, 512), 512)
            part[:, tile] = dot_tn(tab[...], q[:, tile]).astype(BF16)

        s_c[c] = send(part.at[pl.ds(2 * TOK, 2 * TOK), cols], core_recv.at[:, cols], sib)

    def along_z(c):
        cols = pl.ds(c * half_d, half_d)
        s_c[c].wait_recv()
        z_send[:, cols] = (
            part[pl.ds(TOK, TOK), cols].astype(F32)
            + core_recv[pl.ds(TOK, TOK), cols].astype(F32)
        ).astype(BF16)
        z_c[c] = send(z_send.at[:, cols], z_recv.at[:, cols], zp)

    def tokens_out(c):
        cols = pl.ds(c * half_d, half_d)
        z_c[c].wait_recv()
        gout[:, cols] = (
            part[pl.ds(0, TOK), cols].astype(F32)
            + core_recv[pl.ds(0, TOK), cols].astype(F32)
            + z_recv[:, cols].astype(F32)
        ).astype(BF16)
        done.append(local_copy(gout.at[:, cols], out_x.at[:, cols]))

    forward(0)
    send_tokens(*steps[2])
    send_tokens(*steps[3])
    forward(1)
    front(0)
    front(1)
    send_tokens(*steps[4])
    forward(2)
    send_tokens(*steps[5])
    front(2)
    pass_on(*steps[0])
    send_tokens(*steps[6])
    forward(3)
    front(3)
    pass_on(*steps[1])
    forward(4)
    pass_on(*steps[2])
    send_tokens(*steps[7])
    weights_first(2)
    forward(5)
    front(4)
    pass_on(*steps[3])
    weights_second(2)
    front(5)
    gate_up(0)
    forward(7)
    pass_on(*steps[4])
    pass_on(*steps[5])
    gate_up(1)
    forward(6)
    make_hidden()
    front(6)
    grads_down(0)
    grads_down(1)
    pass_on(*steps[6])
    front(7)
    reduce_first(0)
    reduce_first(1)
    reduce_second(0)
    pass_on(*steps[7])
    d_hidden(0)
    elementwise(0, ROWS // 128)
    reduce_second(1)
    grads_down(2)
    gather_first(0)
    grads_down(3)
    d_hidden(1)
    gather_first(1)
    elementwise(ROWS // 128, 2 * ROWS // 128)
    grads(0, 0)
    reduce_first(3)
    send_grads(4)
    reduce_first(2)
    grads(1, 0)
    gather_second(0)
    grads(0, 1)
    send_grads(5)
    reduce_second(3)
    gather_second(1)
    partner_rows(1)
    reduce_second(2)
    reduce_first(4)
    partner_rows(0)
    send_grads(7)
    gather_first(3)
    gather_first(2)
    send_grads(6)
    grads(1, 1)
    finish(0)
    reduce_first(5)
    reduce_second(4)
    reduce_first(6)
    send_partner_rows(0)
    reduce_first(7)
    own_rows()
    gather_second(2)
    reduce_second(5)
    reduce_second(7)
    gather_first(4)
    return_rows(0)
    gather_second(3)
    send_partner_rows(1)
    finish(1)
    reduce_second(6)
    gather_first(5)
    gather_first(7)
    return_rows(1)
    combine(0)
    gather_first(6)
    along_z(0)
    gather_second(4)
    gather_second(5)
    combine(1)
    gather_second(7)
    finish(2)
    along_z(1)
    finish(5)
    finish(7)
    finish(4)
    finish(3)
    gather_second(6)
    tokens_out(0)
    tokens_out(1)
    finish(6)
    for c in done:
        c.wait()
    for c in pending.values():
        c.wait_send()


SCRATCH = (
    ((GN - 1, 8, GT), F32),
    ((2, GT, D), BF16),
    ((ROWS, GT), BF16),
    ((ROWS, 128), F32),
    ((2, XN - 1, CHUNK, D), BF16),
    ((2, 2 * ROWS, D), BF16),
    ((3 * HALF, D), BF16),
    ((2 * ROWS, 2 * HALF), F32),
    ((2 * ROWS, HALF), F32),
    ((2 * ROWS, 2 * HALF), BF16),
    ((6 * BLK, 2 * ROWS), BF16),
    ((3, BLK, D), F32),
    ((3, BLK, D), BF16),
    ((3, BLK, D), BF16),
    ((8, QUART, D // 4), BF16),
    ((8, QUART, D // 4), BF16),
    ((8, QUART, D // 2), BF16),
    ((8, QUART, D // 2), BF16),
    ((3, BLK, D), BF16),
    ((ROWS, D), F32),
    ((ROWS, D), BF16),
    ((ROWS, D), BF16),
    ((ROWS, D), BF16),
    ((GT, D), BF16),
    ((2 * TOK, D), BF16),
    ((TOK, D), BF16),
    ((TOK, D), BF16),
    ((TOK, D), BF16),
)


def local(inputs, upstream, gates, routes, w_gate, w_up, w_down):
    meta = jnp.concatenate(
        [routes.T.astype(F32), gates.T, jnp.zeros((4, TOK), F32)], axis=0
    )
    meta = jnp.tile(meta, (1, GN))
    anywhere = pl.BlockSpec(memory_space=pl.ANY)
    outs = pl.pallas_call(
        kernel,
        out_shape=(
            jax.ShapeDtypeStruct((TOK, D), BF16),
            jax.ShapeDtypeStruct((BLK, D), BF16),
            jax.ShapeDtypeStruct((BLK, D), BF16),
            jax.ShapeDtypeStruct((BLK, D), BF16),
        ),
        in_specs=[pl.BlockSpec(memory_space=pltpu.VMEM)] + [anywhere] * 5,
        out_specs=[anywhere] * 4,
        scratch_shapes=[pltpu.VMEM(shape, dtype) for shape, dtype in SCRATCH]
        + [
            pltpu.SemaphoreType.DMA((NSEM,)),
            pltpu.SemaphoreType.DMA((NSEM,)),
            pltpu.SemaphoreType.DMA((16,)),
        ],
        compiler_params=pltpu.CompilerParams(
            collective_id=0, has_side_effects=True, vmem_limit_bytes=62 * 2**20
        ),
        name="expert_backward",
    )(meta, inputs, upstream, w_gate[0], w_up[0], w_down[0])
    return outs[0], outs[1][None], outs[2][None], outs[3][None]


def solution(mesh):
    tokens = P(("expert", "fsdp", "dp"), None)
    hidden = P("expert", "fsdp", None)
    return jax.shard_map(
        local,
        mesh=mesh,
        in_specs=(tokens, tokens, tokens, tokens, hidden, hidden, hidden),
        out_specs=(tokens, hidden, hidden, hidden),
        check_vma=False,
    )
```
